256 devices in a mesh: region: 8 (over x, core), sub: 32 (over y, z).
Axes of the slice: x: 4, y: 4, z: 8, core: 2. Of those that a mesh axis runs over, the one named last changes fastest.
Arguments:
- block_inverse: bfloat16 [98304, 4096], P(('region', 'sub')), may hold values from -0.75 to 0.75
- probes: bfloat16 [98304, 4096], P(('region', 'sub')), may hold values from -6 to 6
- coupling: bfloat16 [16384, 32768], P(('region', 'sub')), may hold values from -0.25 to 0.25
- columns: int32 [16384, 8], P(('region', 'sub')), may hold values from 0 to 383
- residual: float32 [1048576], P(('region', 'sub')), may hold values from -6 to 6
Outputs:
- basis: float32 [1048576, 64], P(('region', 'sub'))
- correction: float32 [1048576], P(('region', 'sub'))
The draws below stay inside these ranges and needn't reach their ends.
All inputs are finite; a program needn't handle non-finite values.
Results may differ from the reference program's by a relative error of at most 0.0058.
Values may be sent and summed in bfloat16 or wider, within the bound.
No kernel may reach another device: no remote copies, remote signals or barrier semaphores. Data moves between devices by JAX's collectives and lax.ppermute only.
A program may use at most 128 MiB of HBM per device.

```python
import jax
import jax.numpy as jnp
from jax import lax

BLOCK = 64
RANK = 64
NB = 384
NI = 64
KB = 8
BLOCKS = 98304
IBLOCKS = 16384
TOTAL = 1048576
N_REGION = 8
N_SUB = 32


def plant(drawn, key, smallest, high):
    shape = drawn.shape
    index_at = [jax.random.randint(jax.random.fold_in(key, axis), (), 0, shape[axis]) for axis in range(len(shape))]
    drawn = drawn.at[tuple(index_at)].set(smallest)
    longest = shape.index(max(shape))
    index_at[longest] = (index_at[longest] + 1) % shape[longest]
    return drawn.at[tuple(index_at)].set(high)


def levels(rng, shape, cuts, smallest, largest):
    def one(dim, parts):
        draws = jax.random.uniform(jax.random.fold_in(jax.random.fold_in(rng, 6), dim), (parts,), jnp.float32, smallest / len(cuts), largest / len(cuts))
        return jnp.repeat(jnp.exp(draws), shape[dim] // parts).reshape((-1,) + (1,) * (len(shape) - dim - 1))

    gain = one(*cuts[0])
    for cut in cuts[1:]:
        gain = gain * one(*cut)
    return gain


def normal_values(rng, shape, scale, limit, split=(), dtype=jnp.bfloat16):
    level = levels(rng, shape, split, -0.22, 0.18) if split else 1.0
    array = jax.random.normal(rng, shape, jnp.float32) * scale * level
    return jnp.minimum(jnp.maximum(array, -limit), limit).astype(dtype)


def setup_inputs(seed: int = 0) -> dict:
    arg_keys = jax.random.split(jax.random.key(seed), 6)
    return {
        "block_inverse": normal_values(arg_keys[0], (BLOCKS, BLOCK * BLOCK), BLOCK ** -0.5, 0.75, ((0, 256),)),
        "probes": normal_values(arg_keys[1], (BLOCKS, BLOCK * RANK), 1.0, 6.0, ((0, 256),)),
        "coupling": normal_values(arg_keys[2], (IBLOCKS, KB * BLOCK * BLOCK), (BLOCK * KB) ** -0.5, 0.25, ((0, 256),)),
        "columns": plant(jax.random.randint(arg_keys[3], (IBLOCKS, KB), 0, NB), jax.random.fold_in(arg_keys[3], 1), 0, NB - 1).astype(jnp.int32),
        "residual": normal_values(arg_keys[4], (TOTAL,), 1.0, 6.0, ((0, 256),), jnp.float32),
    }


def device_piece(operands):
    block_inverse, probes, coupling, columns = operands
    inverse_blocks = block_inverse.reshape(NB, BLOCK, BLOCK)
    probe_blocks = probes.reshape(NB, BLOCK, RANK)
    coupling_blocks = coupling.reshape(NI, KB, BLOCK, BLOCK)
    solved = jnp.einsum('bij,bjk->bik', inverse_blocks.astype(jnp.float32), probe_blocks.astype(jnp.float32)).astype(jnp.bfloat16)
    picked = solved[columns.astype(jnp.int32)]
    pieces = jnp.einsum('nkij,nkjr->nir', coupling_blocks.astype(jnp.float32), picked.astype(jnp.float32))
    return pieces.astype(jnp.bfloat16).reshape(NI * BLOCK, RANK)

def region_solve(operands):
    owned_rows, residual = operands
    total_rows = owned_rows.shape[0]
    gram_total = jnp.dot(owned_rows.T.astype(jnp.float32), owned_rows.astype(jnp.float32), preferred_element_type=jnp.float32)
    lower_factor = jnp.linalg.cholesky(gram_total)
    basis_t = jax.scipy.linalg.solve_triangular(lower_factor, owned_rows.T.astype(jnp.float32), lower=True)
    coefficients = jnp.dot(basis_t, residual, precision=lax.Precision.HIGHEST)
    basis = jnp.sqrt(jnp.float32(total_rows)) * basis_t.T
    correction = jnp.sqrt(jnp.float32(total_rows) / RANK) * jnp.dot(basis_t.T, coefficients, precision=lax.Precision.HIGHEST)
    return (basis, correction)

def reference(block_inverse, probes, coupling, columns, residual):
    count = N_REGION * N_SUB
    pieces = lax.map(device_piece, (block_inverse.reshape(count, NB, BLOCK * BLOCK), probes.reshape(count, NB, BLOCK * RANK), coupling.reshape(count, NI, KB * BLOCK * BLOCK), columns.reshape(count, NI, KB)))
    run_rows = NI * BLOCK // N_REGION
    owned_rows = pieces.reshape(N_REGION, N_SUB, N_REGION, run_rows, RANK).transpose(2, 1, 0, 3, 4).reshape(N_REGION, N_SUB * NI * BLOCK, RANK)
    basis, correction = lax.map(region_solve, (owned_rows, residual.reshape(N_REGION, N_SUB * NI * BLOCK)))
    return (basis.reshape(TOTAL, RANK), correction.reshape(TOTAL))
```

```python
import functools
import math

import jax
import jax.numpy as jnp
from jax import lax
from jax.experimental import pallas as pl
from jax.experimental.pallas import tpu as pltpu
from jax.sharding import PartitionSpec as P

BLOCK = 64
RANK = 64
ROW = BLOCK * BLOCK
MIB = 2**20


def halves(x, y):
    even = jnp.concatenate([x[:, :BLOCK], y[:, :BLOCK]], axis=1)
    odd = jnp.concatenate([x[:, BLOCK:], y[:, BLOCK:]], axis=1)
    return even, odd


def spread(src, r0, c0, r1, c1, dst, base):
    for p in range(BLOCK // 2):
        x = src[pl.ds(r0, 16), pl.ds(c0 + 128 * p, 128)]
        y = src[pl.ds(r1, 16), pl.ds(c1 + 128 * p, 128)]
        even, odd = halves(x, y)
        dst[pl.ds(base + 32 * p, 16), :] = even.astype(jnp.float32)
        dst[pl.ds(base + 32 * p + 16, 16), :] = odd.astype(jnp.float32)


def pieces_kernel(cols_ref, inv_ref, prb_ref, cpl_ref, out_ref, inv_v, prb_v, cpl_v, stage_a, stage_p, stage_c, solved, sem):
    nb, ni = inv_ref.shape[0], cpl_ref.shape[0]
    kb = cpl_ref.shape[1] // ROW

    def interior_copies(g):
        rows = pl.ds(pl.multiple_of(g * 32, 32), 32)
        return (
            pltpu.make_async_copy(inv_ref.at[rows], inv_v.at[rows], sem.at[0, g]),
            pltpu.make_async_copy(prb_ref.at[rows], prb_v.at[rows], sem.at[1, g]),
        )

    def coupling_copy(g):
        rows = pl.ds(pl.multiple_of(g * 16, 16), 16)
        return pltpu.make_async_copy(cpl_ref.at[rows], cpl_v.at[rows], sem.at[2, g])

    for g in range(nb // 32):
        for copy in interior_copies(g):
            copy.start()
    for g in range(ni // 16):
        coupling_copy(g).start()
    low = lax.broadcasted_iota(jnp.int32, (BLOCK, 128), 1) < BLOCK

    def solve_group(g, carry):
        for copy in interior_copies(g):
            copy.wait()
        r0 = pl.multiple_of(g * 32, 32)
        spread(inv_v, r0, 0, r0 + 16, 0, stage_a, 0)
        spread(prb_v, r0, 0, r0 + 16, 0, stage_p, 0)
        for u in range(16):
            lhs = stage_a[pl.ds(u, BLOCK, stride=16), :].astype(jnp.bfloat16)
            prb = stage_p[pl.ds(u, BLOCK, stride=16), :]
            rhs = jnp.concatenate([jnp.where(low, prb, 0.0), jnp.where(low, 0.0, prb)], axis=0)
            both = jnp.dot(lhs, rhs.astype(jnp.bfloat16), preferred_element_type=jnp.float32)
            both = both.astype(jnp.bfloat16)
            solved[r0 + u] = both
            solved[r0 + 16 + u] = jnp.concatenate([both[:, BLOCK:], both[:, :BLOCK]], axis=1)
        return carry

    lax.fori_loop(0, nb // 32, solve_group, 0)

    def couple_group(g, carry):
        coupling_copy(g).wait()
        r0 = pl.multiple_of(g * 16, 16)
        for kp in range(kb // 2):
            spread(cpl_v, r0, 2 * ROW * kp, r0, 2 * ROW * kp + ROW, stage_c, 16 * BLOCK * kp)
        for up in range(8):
            two = []
            for u in (2 * up, 2 * up + 1):
                lhs = [stage_c[pl.ds(16 * BLOCK * kp + u, BLOCK, stride=16), :].astype(jnp.bfloat16) for kp in range(kb // 2)]
                rhs = [solved[cols_ref[(r0 + u) * kb + k]] for k in range(kb)]
                two.append(jnp.dot(jnp.concatenate(lhs, axis=1), jnp.concatenate(rhs, axis=0), preferred_element_type=jnp.float32))
            turned = jnp.transpose(jnp.concatenate(two, axis=0), (1, 0))[:RANK].astype(jnp.bfloat16)
            out_ref[2 * g + up // 4, :, (up % 4) * 128 : (up % 4) * 128 + 128] = turned
        return carry

    lax.fori_loop(0, ni // 16, couple_group, 0)


def turned_pieces(block_inverse, probes, coupling, columns, regions):
    nb, ni = block_inverse.shape[0], coupling.shape[0]
    any_place = pl.BlockSpec(memory_space=pl.ANY)
    return pl.pallas_call(
        pieces_kernel,
        out_shape=jax.ShapeDtypeStruct((regions, RANK, ni * BLOCK // regions), jnp.bfloat16),
        in_specs=[pl.BlockSpec(memory_space=pltpu.SMEM), any_place, any_place, any_place],
        out_specs=pl.BlockSpec(memory_space=pltpu.VMEM),
        scratch_shapes=[
            pltpu.VMEM(block_inverse.shape, jnp.bfloat16),
            pltpu.VMEM(probes.shape, jnp.bfloat16),
            pltpu.VMEM(coupling.shape, jnp.bfloat16),
            pltpu.VMEM((16 * BLOCK, 128), jnp.float32),
            pltpu.VMEM((16 * BLOCK, 128), jnp.float32),
            pltpu.VMEM((64 * BLOCK, 128), jnp.float32),
            pltpu.VMEM((nb, BLOCK, 128), jnp.bfloat16),
            pltpu.SemaphoreType.DMA((3, nb // 32)),
        ],
        compiler_params=pltpu.CompilerParams(vmem_limit_bytes=60 * MIB),
    )(columns.reshape(-1), block_inverse, probes, coupling)


NT = (((1,), (1,)), ((), ()))


def three_parts(x):
    high = x.astype(jnp.bfloat16)
    rest = x - high.astype(jnp.float32)
    middle = rest.astype(jnp.bfloat16)
    low = (rest - middle.astype(jnp.float32)).astype(jnp.bfloat16)
    return jnp.concatenate([high, middle, low], axis=0)


def gram_kernel(rows_ref, res_ref, out_ref):
    regions, rank, run = rows_ref.shape
    gram = jnp.zeros((rank, rank), jnp.float32)
    moment = jnp.zeros((3, rank), jnp.float32)
    for r in range(regions):
        y = rows_ref[r]
        gram += lax.dot_general(y, y, NT, preferred_element_type=jnp.float32)
        parts = three_parts(res_ref[:, r * run : (r + 1) * run])
        moment += lax.dot_general(parts, y, NT, preferred_element_type=jnp.float32)
    half = rank // 2
    out_ref[:half, :] = jnp.concatenate([gram[:half], gram[half:]], axis=1)
    row = moment[0:1] + moment[1:2] + moment[2:3]
    row = jnp.concatenate([row, jnp.zeros_like(row)], axis=1)
    out_ref[half:, :] = jnp.broadcast_to(row, (8, 2 * rank))


def finish_kernel(total_rows, sum_ref, rows_ref, basis_ref, corr_ref, basis_v, sem):
    regions, rank, run = rows_ref.shape
    half = rank // 2
    packed = sum_ref[:half, :]
    gram = jnp.concatenate([packed[:, :rank], packed[:, rank:]], axis=0)
    moment = sum_ref[half : half + 1, :rank]
    row_at = lax.broadcasted_iota(jnp.int32, (rank, 2 * rank), 0)
    lane_at = lax.broadcasted_iota(jnp.int32, (rank, 2 * rank), 1)
    one = (lane_at == row_at + rank).astype(jnp.float32)
    m = jnp.concatenate([gram, jnp.zeros_like(gram)], axis=1) + one
    for k in range(rank):
        pivot_row = m[k : k + 1, :]
        inverse = 1.0 / pivot_row[:, k : k + 1]
        column = jnp.broadcast_to(m[:, k : k + 1], (rank, 2 * rank))
        factor = jnp.where(row_at > k, column, 0.0) * inverse
        m = m - factor * pivot_row
    diagonal = jnp.sum(jnp.where(row_at == lane_at, m, 0.0), axis=1, keepdims=True)
    lower_inverse = m[:, rank:] * (1.0 / jnp.sqrt(diagonal))
    coefficients = jnp.sum(lower_inverse * moment, axis=1, keepdims=True)
    scale = math.sqrt(total_rows)
    weights = three_parts(lower_inverse * scale)
    weights = weights[: 2 * rank]
    shrink = 1.0 / math.sqrt(rank)

    def copy_out(r):
        cols = pl.ds(r * run, run)
        return pltpu.make_async_copy(basis_v.at[:, cols], basis_ref.at[:, cols], sem.at[r])

    for r in range(regions):
        q = jnp.dot(weights, rows_ref[r], preferred_element_type=jnp.float32)
        q = q[:rank] + q[rank:]
        basis_v[:, r * run : (r + 1) * run] = q
        copy_out(r).start()
        corr_ref[:, r * run : (r + 1) * run] = jnp.sum(q * (coefficients * shrink), axis=0, keepdims=True)
    for r in range(regions):
        copy_out(r).wait()


def per_device(block_inverse, probes, coupling, columns, residual):
    regions, subs = lax.axis_size("region"), lax.axis_size("sub")
    rows_here = residual.shape[0]
    in_vmem = pl.BlockSpec(memory_space=pltpu.VMEM)
    pieces = turned_pieces(block_inverse, probes, coupling, columns, regions)
    owned = lax.all_to_all(pieces, "region", split_axis=0, concat_axis=0, tiled=True)
    total = pl.pallas_call(
        gram_kernel,
        out_shape=jax.ShapeDtypeStruct((RANK // 2 + 8, 2 * RANK), jnp.float32),
        in_specs=[in_vmem, in_vmem],
        out_specs=in_vmem,
    )(owned, residual.reshape(1, rows_here))
    for step in (8, 24, 1, 6, 2):
        total = total + lax.ppermute(total, "sub", [(i, i ^ step) for i in range(subs)])
    basis_t, correction = pl.pallas_call(
        functools.partial(finish_kernel, rows_here * subs),
        out_shape=(
            jax.ShapeDtypeStruct((RANK, rows_here), jnp.float32),
            jax.ShapeDtypeStruct((1, rows_here), jnp.float32),
        ),
        in_specs=[in_vmem, in_vmem],
        out_specs=(pl.BlockSpec(memory_space=pl.ANY), in_vmem),
        scratch_shapes=[pltpu.VMEM((RANK, rows_here), jnp.float32), pltpu.SemaphoreType.DMA((regions,))],
    )(total, owned)
    return basis_t.T, correction.reshape(rows_here)


def solution(mesh):
    blocks = P(("region", "sub"), None)
    rows = P(("region", "sub"))
    return jax.shard_map(
        per_device,
        mesh=mesh,
        in_specs=(blocks, blocks, blocks, blocks, rows),
        out_specs=(blocks, rows),
        check_vma=False,
    )
```

```python
import functools
import math

import jax
import jax.numpy as jnp
from jax import lax
from jax.experimental import pallas as pl
from jax.experimental.pallas import tpu as pltpu
from jax.sharding import PartitionSpec as P

BLOCK = 64
RANK = 64
ROW = BLOCK * BLOCK
MIB = 2**20
STEP = 8
NT = (((1,), (1,)), ((), ()))


def spread(src, r0, c0, r1, c1, dst, base, p):
    x = src[pl.ds(r0, 16), pl.ds(c0 + 128 * p, 128)]
    y = src[pl.ds(r1, 16), pl.ds(c1 + 128 * p, 128)]
    even = jnp.concatenate([x[:, :BLOCK], y[:, :BLOCK]], axis=1).astype(jnp.float32)
    odd = jnp.concatenate([x[:, BLOCK:], y[:, BLOCK:]], axis=1).astype(jnp.float32)
    for h in range(2):
        at = base + 8 * BLOCK * h + 16 * p
        dst[pl.ds(at, 8), :] = even[8 * h : 8 * h + 8]
        dst[pl.ds(at + 8, 8), :] = odd[8 * h : 8 * h + 8]

def gathered(stage, base, u):
    return stage[pl.ds(base + u // 8 * 8 * BLOCK + u % 8, BLOCK, stride=8), :]

def pieces_kernel(cols_hbm, inv_ref, prb_ref, cpl_ref, out_ref, cols, inv_v, prb_v, cpl_v, a0, a1, p0, p1, c0, c1, solved, sem, cols_sem):
    nb, ni = inv_ref.shape[0], cpl_ref.shape[0]
    kb = cpl_ref.shape[1] // ROW
    groups, cgroups = nb // 32, ni // 16

    def interior_copies(g):
        rows = pl.ds(pl.multiple_of(g * 32, 32), 32)
        return (
            pltpu.make_async_copy(inv_ref.at[rows], inv_v.at[rows], sem.at[0, g]),
            pltpu.make_async_copy(prb_ref.at[rows], prb_v.at[rows], sem.at[1, g]),
        )

    def coupling_copy(g):
        rows = pl.ds(pl.multiple_of(g * 16, 16), 16)
        return pltpu.make_async_copy(cpl_ref.at[rows], cpl_v.at[rows], sem.at[2, g])

    cols_copy = pltpu.make_async_copy(cols_hbm, cols, cols_sem)
    for copy in interior_copies(0):
        copy.start()
    cols_copy.start()
    for g in range(1, groups):
        for copy in interior_copies(g):
            copy.start()
    for g in range(cgroups):
        coupling_copy(g).start()
    low = lax.broadcasted_iota(jnp.int32, (BLOCK, 128), 1) < BLOCK

    def solve_spread(g, sa, sp, p):
        r0 = pl.multiple_of(g * 32, 32)
        spread(inv_v, r0, 0, r0 + 16, 0, sa, 0, p)
        spread(prb_v, r0, 0, r0 + 16, 0, sp, 0, p)

    def solve(g, sa, sp, u):
        r0 = g * 32
        lhs = gathered(sa, 0, u).astype(jnp.bfloat16)
        prb = gathered(sp, 0, u)
        rhs = jnp.concatenate([jnp.where(low, prb, 0.0), jnp.where(low, 0.0, prb)], axis=0)
        both = jnp.dot(lhs, rhs.astype(jnp.bfloat16), preferred_element_type=jnp.float32)
        both = both.astype(jnp.bfloat16)
        solved[r0 + u] = both
        solved[r0 + 16 + u] = jnp.concatenate([both[:, BLOCK:], both[:, :BLOCK]], axis=1)

    def couple_spread(g, sc, q):
        kp, p = q // 32, q % 32
        r0 = pl.multiple_of(g * 16, 16)
        spread(cpl_v, r0, 2 * ROW * kp, r0, 2 * ROW * kp + ROW, sc, 16 * BLOCK * kp, p)

    def couple(g, sc, up):
        two = []
        for u in (2 * up, 2 * up + 1):
            lhs = [gathered(sc, 16 * BLOCK * kp, u).astype(jnp.bfloat16) for kp in range(kb // 2)]
            rhs = [solved[cols[k, g * 16 + u]] for k in range(kb)]
            two.append(jnp.dot(jnp.concatenate(lhs, axis=1), jnp.concatenate(rhs, axis=0), preferred_element_type=jnp.float32))
        turned = jnp.transpose(jnp.concatenate(two, axis=0).astype(jnp.bfloat16), (1, 0))[:RANK]
        out_ref[2 * g + up // 4, :, (up % 4) * 128 : (up % 4) * 128 + 128] = turned

    def wait(g):
        for copy in interior_copies(g):
            copy.wait()

    def solve_beside(g, sa, sp, na, np_):
        wait(g + 1)
        for u in range(16):
            solve(g, sa, sp, u)
            for p in (2 * u, 2 * u + 1):
                solve_spread(g + 1, na, np_, p)

    wait(0)
    for p in range(32):
        solve_spread(0, a0, p0, p)

    def two_groups(t, carry):
        solve_beside(2 * t, a0, p0, a1, p1)
        solve_beside(2 * t + 1, a1, p1, a0, p0)
        return carry

    lax.fori_loop(0, groups // 2 - 1, two_groups, 0)
    solve_beside(groups - 2, a0, p0, a1, p1)
    coupling_copy(0).wait()
    for u in range(16):
        solve(groups - 1, a1, p1, u)
        for q in range(8 * u, 8 * u + 8):
            couple_spread(0, c0, q)
    cols_copy.wait()
    for g in range(cgroups):
        here, there = (c0, c1) if g % 2 == 0 else (c1, c0)
        if g + 1 < cgroups:
            coupling_copy(g + 1).wait()
        for up in range(8):
            couple(g, here, up)
            if g + 1 < cgroups:
                for q in range(16 * up, 16 * up + 16):
                    couple_spread(g + 1, there, q)


def turned_pieces(block_inverse, probes, coupling, columns, regions):
    nb, ni = block_inverse.shape[0], coupling.shape[0]
    any_place = pl.BlockSpec(memory_space=pl.ANY)
    stage = pltpu.VMEM((16 * BLOCK, 128), jnp.float32)
    big = pltpu.VMEM((64 * BLOCK, 128), jnp.float32)
    return pl.pallas_call(
        pieces_kernel,
        out_shape=jax.ShapeDtypeStruct((regions, RANK, ni * BLOCK // regions), jnp.bfloat16),
        in_specs=[any_place] * 4,
        out_specs=pl.BlockSpec(memory_space=pltpu.VMEM),
        scratch_shapes=[
            pltpu.SMEM(columns.shape[::-1], jnp.int32),
            pltpu.VMEM(block_inverse.shape, jnp.bfloat16),
            pltpu.VMEM(probes.shape, jnp.bfloat16),
            pltpu.VMEM(coupling.shape, jnp.bfloat16),
            stage, stage, stage, stage, big, big,
            pltpu.VMEM((nb, BLOCK, 128), jnp.bfloat16),
            pltpu.SemaphoreType.DMA((3, nb // 32)),
            pltpu.SemaphoreType.DMA(()),
        ],
        compiler_params=pltpu.CompilerParams(vmem_limit_bytes=58 * MIB),
    )(columns.T, block_inverse, probes, coupling)


def three_parts(x):
    high = x.astype(jnp.bfloat16)
    rest = x - high.astype(jnp.float32)
    middle = rest.astype(jnp.bfloat16)
    low = (rest - middle.astype(jnp.float32)).astype(jnp.bfloat16)
    return jnp.concatenate([high, middle, low], axis=0)


def gram_kernel(rows_ref, res_ref, out_ref):
    regions, rank, run = rows_ref.shape
    gram = jnp.zeros((rank, rank), jnp.float32)
    moment = jnp.zeros((3, rank), jnp.float32)
    for r in range(regions):
        y = rows_ref[r]
        gram += lax.dot_general(y, y, NT, preferred_element_type=jnp.float32)
        parts = three_parts(res_ref[:, r * run : (r + 1) * run])
        moment += lax.dot_general(parts, y, NT, preferred_element_type=jnp.float32)
    half = rank // 2
    out_ref[:half, :] = jnp.concatenate([gram[:half], gram[half:]], axis=1)
    row = moment[0:1] + moment[1:2] + moment[2:3]
    row = jnp.concatenate([row, jnp.zeros_like(row)], axis=1)
    out_ref[half:, :] = jnp.broadcast_to(row, (8, 2 * rank))


def two_parts(x):
    high = x.astype(jnp.bfloat16)
    return jnp.concatenate([high, (x - high.astype(jnp.float32)).astype(jnp.bfloat16)], axis=0)


def inverse_lower(gram):
    rank = gram.shape[0]
    row_at = lax.broadcasted_iota(jnp.int32, (rank, 2 * rank), 0)
    lane_at = lax.broadcasted_iota(jnp.int32, (rank, 2 * rank), 1)
    rest = jnp.concatenate([gram, jnp.zeros_like(gram)], axis=1) + (lane_at == row_at + rank).astype(jnp.float32)
    done = []
    for k in range(0, rank, STEP):
        at = row_at[: rank - k]
        cols = [jnp.broadcast_to(rest[:, k + j : k + j + 1], rest.shape) for j in range(STEP)]
        rows = [rest[j : j + 1, :] for j in range(STEP)]
        pivots = []
        for j in range(STEP):
            pivot = cols[j][j : j + 1, :]
            pivots.append(pivot)
            factor = jnp.where(at > j, cols[j] * (1.0 / pivot), 0.0)
            for l in range(j + 1, STEP):
                cols[l] = cols[l] - factor * cols[l][j : j + 1, :]
                rows[l] = rows[l] - factor[l : l + 1, :] * rows[j]
            rest = rest - factor * rows[j]
        done.append(rest[:STEP, rank:] * lax.rsqrt(jnp.concatenate(pivots, axis=0)[:, :rank]))
        rest = rest[STEP:]
    return jnp.concatenate(done, axis=0)


def finish_kernel(total_rows, sum_ref, more_ref, rows_ref, basis_ref, corr_ref, basis_v, sem):
    regions, rank, run = rows_ref.shape
    half = rank // 2
    total = sum_ref[...] + more_ref[...]
    packed = total[:half]
    gram = jnp.concatenate([packed[:, :rank], packed[:, rank:]], axis=0)
    moment = total[half : half + 1, :rank]
    lower_inverse = inverse_lower(gram)
    coefficients = jnp.sum(lower_inverse * moment, axis=1, keepdims=True)
    weights = two_parts(lower_inverse * math.sqrt(total_rows))
    shrink = 1.0 / math.sqrt(rank)

    def copy_out(r):
        cols = pl.ds(r * run, run)
        return pltpu.make_async_copy(basis_v.at[:, cols], basis_ref.at[:, cols], sem.at[r])

    for r in range(regions):
        q = jnp.dot(weights, rows_ref[r], preferred_element_type=jnp.float32)
        q = q[:rank] + q[rank:]
        basis_v[:, r * run : (r + 1) * run] = q
        copy_out(r).start()
        corr_ref[:, r * run : (r + 1) * run] = jnp.sum(q * (coefficients * shrink), axis=0, keepdims=True)
    for r in range(regions):
        copy_out(r).wait()


def per_device(block_inverse, probes, coupling, columns, residual):
    regions, subs = lax.axis_size("region"), lax.axis_size("sub")
    rows_here = residual.shape[0]
    in_vmem = pl.BlockSpec(memory_space=pltpu.VMEM)
    pieces = turned_pieces(block_inverse, probes, coupling, columns, regions)
    owned = lax.all_to_all(pieces, "region", split_axis=0, concat_axis=0, tiled=True)
    total = pl.pallas_call(
        gram_kernel,
        out_shape=jax.ShapeDtypeStruct((RANK // 2 + 8, 2 * RANK), jnp.float32),
        in_specs=[in_vmem, in_vmem],
        out_specs=in_vmem,
        compiler_params=pltpu.CompilerParams(vmem_limit_bytes=16 * MIB),
    )(owned, residual.reshape(1, rows_here))
    more = jnp.zeros_like(total)
    for n, step in enumerate((8, 24, 1, 6, 2)):
        total = total + more if n else total
        more = lax.ppermute(total, "sub", [(i, i ^ step) for i in range(subs)])
    basis_t, correction = pl.pallas_call(
        functools.partial(finish_kernel, rows_here * subs),
        out_shape=(
            jax.ShapeDtypeStruct((RANK, rows_here), jnp.float32),
            jax.ShapeDtypeStruct((1, rows_here), jnp.float32),
        ),
        in_specs=[in_vmem, in_vmem, in_vmem],
        out_specs=(pl.BlockSpec(memory_space=pl.ANY), in_vmem),
        scratch_shapes=[pltpu.VMEM((RANK, rows_here), jnp.float32), pltpu.SemaphoreType.DMA((regions,))],
        compiler_params=pltpu.CompilerParams(vmem_limit_bytes=16 * MIB),
    )(total, more, owned)
    return basis_t.T, correction.reshape(rows_here)


def solution(mesh):
    blocks = P(("region", "sub"), None)
    rows = P(("region", "sub"))
    return jax.shard_map(
        per_device,
        mesh=mesh,
        in_specs=(blocks, blocks, blocks, blocks, rows),
        out_specs=(blocks, rows),
        check_vma=False,
    )
```

```python
import functools
import math

import jax
import jax.numpy as jnp
from jax import lax
from jax.experimental import pallas as pl
from jax.experimental.pallas import tpu as pltpu
from jax.sharding import PartitionSpec as P

BLOCK = 64
RANK = 64
ROW = BLOCK * BLOCK
MIB = 2**20
STEP = 8
NT = (((1,), (1,)), ((), ()))


def spread(src, r0, c0, r1, c1, dst, base, p):
    x = src[pl.ds(r0, 16), pl.ds(c0 + 128 * p, 128)]
    y = src[pl.ds(r1, 16), pl.ds(c1 + 128 * p, 128)]
    even = jnp.concatenate([x[:, :BLOCK], y[:, :BLOCK]], axis=1).astype(jnp.float32)
    odd = jnp.concatenate([x[:, BLOCK:], y[:, BLOCK:]], axis=1).astype(jnp.float32)
    for h in range(2):
        at = base + 8 * BLOCK * h + 16 * p
        dst[pl.ds(at, 8), :] = even[8 * h : 8 * h + 8]
        dst[pl.ds(at + 8, 8), :] = odd[8 * h : 8 * h + 8]

def gathered(stage, base, u):
    return stage[pl.ds(base + u // 8 * 8 * BLOCK + u % 8, BLOCK, stride=8), :]

def pieces_kernel(cols_hbm, inv_ref, prb_ref, cpl_ref, out_ref, cols, inv_v, prb_v, cpl_v, a0, a1, p0, p1, c0, c1, solved, out_v, sem, cols_sem, out_sem):
    nb, ni = inv_ref.shape[0], cpl_ref.shape[0]
    kb = cpl_ref.shape[1] // ROW
    groups, cgroups = nb // 32, ni // 16

    def interior_copies(g):
        rows = pl.ds(pl.multiple_of(g * 32, 32), 32)
        return (
            pltpu.make_async_copy(inv_ref.at[rows], inv_v.at[rows], sem.at[0, g]),
            pltpu.make_async_copy(prb_ref.at[rows], prb_v.at[rows], sem.at[1, g]),
        )

    def coupling_copy(g):
        rows = pl.ds(pl.multiple_of(g * 16, 16), 16)
        return pltpu.make_async_copy(cpl_ref.at[rows], cpl_v.at[rows], sem.at[2, g])

    cols_copy = pltpu.make_async_copy(cols_hbm, cols, cols_sem)
    for copy in interior_copies(0):
        copy.start()
    cols_copy.start()
    for g in range(1, groups):
        for copy in interior_copies(g):
            copy.start()
    for g in range(cgroups):
        coupling_copy(g).start()
    low = lax.broadcasted_iota(jnp.int32, (BLOCK, 128), 1) < BLOCK

    def solve_spread(g, sa, sp, p):
        r0 = pl.multiple_of(g * 32, 32)
        spread(inv_v, r0, 0, r0 + 16, 0, sa, 0, p)
        spread(prb_v, r0, 0, r0 + 16, 0, sp, 0, p)

    def solve(g, sa, sp, u):
        r0 = g * 32
        lhs = gathered(sa, 0, u).astype(jnp.bfloat16)
        prb = gathered(sp, 0, u)
        rhs = jnp.concatenate([jnp.where(low, prb, 0.0), jnp.where(low, 0.0, prb)], axis=0)
        both = jnp.dot(lhs, rhs.astype(jnp.bfloat16), preferred_element_type=jnp.float32)
        both = both.astype(jnp.bfloat16)
        solved[r0 + u] = both
        solved[r0 + 16 + u] = jnp.concatenate([both[:, BLOCK:], both[:, :BLOCK]], axis=1)

    def couple_spread(g, sc, q):
        kp, p = q // 32, q % 32
        r0 = pl.multiple_of(g * 16, 16)
        spread(cpl_v, r0, 2 * ROW * kp, r0, 2 * ROW * kp + ROW, sc, 16 * BLOCK * kp, p)

    def couple(g, sc, up):
        two = []
        for u in (2 * up, 2 * up + 1):
            lhs = [gathered(sc, 16 * BLOCK * kp, u).astype(jnp.bfloat16) for kp in range(kb // 2)]
            rhs = [solved[cols[k, g * 16 + u]] for k in range(kb)]
            two.append(jnp.dot(jnp.concatenate(lhs, axis=1), jnp.concatenate(rhs, axis=0), preferred_element_type=jnp.float32))
        turned = jnp.transpose(jnp.concatenate(two, axis=0).astype(jnp.bfloat16), (1, 0))[:RANK]
        out_v[2 * g + up // 4, :, (up % 4) * 128 : (up % 4) * 128 + 128] = turned

    def out_copy(g):
        return pltpu.make_async_copy(out_v.at[pl.ds(2 * g, 2)], out_ref.at[pl.ds(2 * g, 2)], out_sem.at[g])

    def wait(g):
        for copy in interior_copies(g):
            copy.wait()

    def solve_beside(g, sa, sp, na, np_):
        for u in range(16):
            solve(g, sa, sp, u)
            for p in (2 * u, 2 * u + 1):
                solve_spread(g + 1, na, np_, p)

    wait(0)
    for p in range(32):
        solve_spread(0, a0, p0, p)

    def two_groups(t, carry):
        wait(2 * t + 1)
        wait(2 * t + 2)
        solve_beside(2 * t, a0, p0, a1, p1)
        solve_beside(2 * t + 1, a1, p1, a0, p0)
        return carry

    lax.fori_loop(0, groups // 2 - 1, two_groups, 0)
    wait(groups - 1)
    for g in range(cgroups):
        coupling_copy(g).wait()
    cols_copy.wait()
    solve_beside(groups - 2, a0, p0, a1, p1)
    for u in range(16):
        solve(groups - 1, a1, p1, u)
        for q in range(8 * u, 8 * u + 8):
            couple_spread(0, c0, q)
    for g in range(cgroups):
        here, there = (c0, c1) if g % 2 == 0 else (c1, c0)
        for up in range(8):
            couple(g, here, up)
            if g + 1 < cgroups:
                for q in range(16 * up, 16 * up + 16):
                    couple_spread(g + 1, there, q)
        out_copy(g).start()
    for g in range(cgroups):
        out_copy(g).wait()


def turned_pieces(block_inverse, probes, coupling, columns, regions):
    nb, ni = block_inverse.shape[0], coupling.shape[0]
    any_place = pl.BlockSpec(memory_space=pl.ANY)
    stage = pltpu.VMEM((16 * BLOCK, 128), jnp.float32)
    big = pltpu.VMEM((64 * BLOCK, 128), jnp.float32)
    return pl.pallas_call(
        pieces_kernel,
        out_shape=jax.ShapeDtypeStruct((regions, RANK, ni * BLOCK // regions), jnp.bfloat16),
        in_specs=[any_place] * 4,
        out_specs=any_place,
        scratch_shapes=[
            pltpu.SMEM(columns.shape[::-1], jnp.int32),
            pltpu.VMEM(block_inverse.shape, jnp.bfloat16),
            pltpu.VMEM(probes.shape, jnp.bfloat16),
            pltpu.VMEM(coupling.shape, jnp.bfloat16),
            stage, stage, stage, stage, big, big,
            pltpu.VMEM((nb, BLOCK, 128), jnp.bfloat16),
            pltpu.VMEM((regions, RANK, ni * BLOCK // regions), jnp.bfloat16),
            pltpu.SemaphoreType.DMA((3, nb // 32)),
            pltpu.SemaphoreType.DMA(()),
            pltpu.SemaphoreType.DMA((ni // 16,)),
        ],
        compiler_params=pltpu.CompilerParams(vmem_limit_bytes=58 * MIB),
    )(columns.T, block_inverse, probes, coupling)


def three_parts(x):
    high = x.astype(jnp.bfloat16)
    rest = x - high.astype(jnp.float32)
    middle = rest.astype(jnp.bfloat16)
    low = (rest - middle.astype(jnp.float32)).astype(jnp.bfloat16)
    return jnp.concatenate([high, middle, low], axis=0)


def packed_sums(gram, moment):
    half = gram.shape[0] // 2
    row_at = lax.broadcasted_iota(jnp.int32, (half, half), 0)
    lane_at = lax.broadcasted_iota(jnp.int32, (half, half), 1)
    first, corner, second = gram[:half, :half], gram[:half, half:], gram[half:, half:]
    square = jnp.concatenate([jnp.where(lane_at >= row_at, first, second), corner], axis=1)
    diagonal = jnp.sum(jnp.where(lane_at == row_at, second, 0.0), axis=0, keepdims=True)
    last = jnp.concatenate([moment, diagonal, jnp.zeros_like(diagonal)], axis=1)
    last = jnp.broadcast_to(last, (8, 4 * half))
    return jnp.concatenate([jnp.concatenate([square[: half // 2], square[half // 2 :]], axis=1), last], axis=0)


def unpacked_sums(packed):
    half = packed.shape[1] // 4
    rank = 2 * half
    row_at = lax.broadcasted_iota(jnp.int32, (half, half), 0)
    lane_at = lax.broadcasted_iota(jnp.int32, (half, half), 1)
    square = jnp.concatenate([packed[: half // 2, :rank], packed[: half // 2, rank:]], axis=0)
    turned = jnp.transpose(jnp.concatenate([square, square], axis=1), (1, 0))
    upper, lower = square[:, :half], turned[:half]
    moment, diagonal = packed[half // 2 : half // 2 + 1, :rank], packed[half // 2 : half // 2 + 1, rank : rank + half]
    first = jnp.where(lane_at >= row_at, upper, lower)
    second = jnp.where(lane_at >= row_at, lower, upper)
    second = jnp.where(lane_at == row_at, diagonal, second)
    top = jnp.concatenate([first, square[:, half:]], axis=1)
    return jnp.concatenate([top, jnp.concatenate([turned[half:rank], second], axis=1)], axis=0), moment


def gram_kernel(rows_ref, res_ref, out_ref):
    regions, rank, run = rows_ref.shape
    gram = jnp.zeros((rank, rank), jnp.float32)
    moment = jnp.zeros((3, rank), jnp.float32)
    for r in range(regions):
        y = rows_ref[r]
        gram += lax.dot_general(y, y, NT, preferred_element_type=jnp.float32)
        parts = three_parts(res_ref[:, r * run : (r + 1) * run])
        moment += lax.dot_general(parts, y, NT, preferred_element_type=jnp.float32)
    packed = packed_sums(gram, moment[0:1] + moment[1:2] + moment[2:3])
    for s in range(out_ref.shape[0]):
        out_ref[s] = packed


def two_parts(x):
    high = x.astype(jnp.bfloat16)
    return jnp.concatenate([high, (x - high.astype(jnp.float32)).astype(jnp.bfloat16)], axis=0)


def inverse_lower(gram):
    rank = gram.shape[0]
    row_at = lax.broadcasted_iota(jnp.int32, (rank, 2 * rank), 0)
    lane_at = lax.broadcasted_iota(jnp.int32, (rank, 2 * rank), 1)
    rest = jnp.concatenate([gram, jnp.zeros_like(gram)], axis=1) + (lane_at == row_at + rank).astype(jnp.float32)
    done = []
    for k in range(0, rank, STEP):
        at = row_at[: rank - k]
        cols = [jnp.broadcast_to(rest[:, k + j : k + j + 1], rest.shape) for j in range(STEP)]
        rows = [rest[j : j + 1, :] for j in range(STEP)]
        pivots = []
        for j in range(STEP):
            pivot = cols[j][j : j + 1, :]
            pivots.append(pivot)
            factor = jnp.where(at > j, cols[j] * (1.0 / pivot), 0.0)
            for l in range(j + 1, STEP):
                cols[l] = cols[l] - factor * cols[l][j : j + 1, :]
                rows[l] = rows[l] - factor[l : l + 1, :] * rows[j]
            rest = rest - factor * rows[j]
        done.append(rest[:STEP, rank:] * lax.rsqrt(jnp.concatenate(pivots, axis=0)[:, :rank]))
        rest = rest[STEP:]
    return jnp.concatenate(done, axis=0)


def finish_kernel(total_rows, sums_ref, rows_ref, basis_ref, corr_ref, basis_v, sem):
    regions, rank, run = rows_ref.shape
    total = sums_ref[0]
    for n in range(1, sums_ref.shape[0]):
        total = total + sums_ref[n]
    gram, moment = unpacked_sums(total)
    lower_inverse = inverse_lower(gram)
    coefficients = jnp.sum(lower_inverse * moment, axis=1, keepdims=True)
    weights = two_parts(lower_inverse * math.sqrt(total_rows))
    shrink = 1.0 / math.sqrt(rank)

    def copy_out(r):
        cols = pl.ds(r * run, run)
        return pltpu.make_async_copy(basis_v.at[:, cols], basis_ref.at[:, cols], sem.at[r])

    for r in range(regions):
        q = jnp.dot(weights, rows_ref[r], preferred_element_type=jnp.float32)
        q = q[:rank] + q[rank:]
        basis_v[:, r * run : (r + 1) * run] = q
        copy_out(r).start()
        corr_ref[:, r * run : (r + 1) * run] = jnp.sum(q * (coefficients * shrink), axis=0, keepdims=True)
    for r in range(regions):
        copy_out(r).wait()


def per_device(block_inverse, probes, coupling, columns, residual):
    regions, subs = lax.axis_size("region"), lax.axis_size("sub")
    rows_here = residual.shape[0]
    in_vmem = pl.BlockSpec(memory_space=pltpu.VMEM)
    pieces = turned_pieces(block_inverse, probes, coupling, columns, regions)
    owned = lax.all_to_all(pieces, "region", split_axis=0, concat_axis=0, tiled=True)
    sums = pl.pallas_call(
        gram_kernel,
        out_shape=jax.ShapeDtypeStruct((subs, RANK // 4 + 8, 2 * RANK), jnp.float32),
        in_specs=[in_vmem, in_vmem],
        out_specs=in_vmem,
        compiler_params=pltpu.CompilerParams(vmem_limit_bytes=16 * MIB),
    )(owned, residual.reshape(1, rows_here))
    sums = lax.all_to_all(sums, "sub", split_axis=0, concat_axis=0, tiled=True)
    basis_t, correction = pl.pallas_call(
        functools.partial(finish_kernel, rows_here * subs),
        out_shape=(
            jax.ShapeDtypeStruct((RANK, rows_here), jnp.float32),
            jax.ShapeDtypeStruct((1, rows_here), jnp.float32),
        ),
        in_specs=[in_vmem, in_vmem],
        out_specs=(pl.BlockSpec(memory_space=pl.ANY), in_vmem),
        scratch_shapes=[pltpu.VMEM((RANK, rows_here), jnp.float32), pltpu.SemaphoreType.DMA((regions,))],
        compiler_params=pltpu.CompilerParams(vmem_limit_bytes=16 * MIB),
    )(sums, owned)
    return basis_t.T, correction.reshape(rows_here)


def solution(mesh):
    blocks = P(("region", "sub"), None)
    rows = P(("region", "sub"))
    return jax.shard_map(
        per_device,
        mesh=mesh,
        in_specs=(blocks, blocks, blocks, blocks, rows),
        out_specs=(blocks, rows),
        check_vma=False,
    )
```

```python
import functools
import math

import jax
import jax.numpy as jnp
from jax import lax
from jax.experimental import pallas as pl
from jax.experimental.pallas import tpu as pltpu
from jax.sharding import PartitionSpec as P

BLOCK = 64
RANK = 64
ROW = BLOCK * BLOCK
MIB = 2**20
STEP = 8


def spread(src, r0, c0, r1, c1, dst, base, p):
    x = src[pl.ds(r0, 16), pl.ds(c0 + 128 * p, 256)]
    y = src[pl.ds(r1, 16), pl.ds(c1 + 128 * p, 256)]
    x = [x[:, BLOCK * i : BLOCK * i + BLOCK] for i in range(4)]
    y = [y[:, BLOCK * i : BLOCK * i + BLOCK] for i in range(4)]
    even = jnp.concatenate([x[0], y[0], x[2], y[2]], axis=1).astype(jnp.float32)
    odd = jnp.concatenate([x[1], y[1], x[3], y[3]], axis=1).astype(jnp.float32)
    for h in range(2):
        for q in range(2):
            at = base + 8 * BLOCK * h + 16 * (p + q)
            dst[pl.ds(at, 8), :] = even[8 * h : 8 * h + 8, 128 * q : 128 * q + 128]
            dst[pl.ds(at + 8, 8), :] = odd[8 * h : 8 * h + 8, 128 * q : 128 * q + 128]


def gathered(stage, base, u):
    return stage[pl.ds(base + u // 8 * 8 * BLOCK + u % 8, BLOCK, stride=8), :]


def pieces_kernel(cols_hbm, inv_ref, prb_ref, cpl_ref, out_ref, cols, inv_v, prb_v, cpl_v, a0, a1, p0, p1, c0, c1, solved, out_v, sem, cols_sem, out_sem):
    nb, ni = inv_ref.shape[0], cpl_ref.shape[0]
    kb = cpl_ref.shape[1] // ROW
    groups, cgroups = nb // 32, ni // 16

    def interior_copies(g):
        rows = pl.ds(pl.multiple_of(g * 32, 32), 32)
        return (
            pltpu.make_async_copy(inv_ref.at[rows], inv_v.at[rows], sem.at[0, g]),
            pltpu.make_async_copy(prb_ref.at[rows], prb_v.at[rows], sem.at[1, g]),
        )

    def coupling_copy(g):
        rows = pl.ds(pl.multiple_of(g * 16, 16), 16)
        return pltpu.make_async_copy(cpl_ref.at[rows], cpl_v.at[rows], sem.at[2, g])

    cols_copy = pltpu.make_async_copy(cols_hbm, cols, cols_sem)
    for copy in interior_copies(0):
        copy.start()
    cols_copy.start()
    for g in range(1, groups):
        for copy in interior_copies(g):
            copy.start()
    for g in range(cgroups):
        coupling_copy(g).start()
    low = lax.broadcasted_iota(jnp.int32, (BLOCK, 128), 1) < BLOCK

    def solve_spread(g, sa, sp, p):
        r0 = pl.multiple_of(g * 32, 32)
        spread(inv_v, r0, 0, r0 + 16, 0, sa, 0, p)
        spread(prb_v, r0, 0, r0 + 16, 0, sp, 0, p)

    def solve(g, sa, sp, u):
        r0 = g * 32
        lhs = gathered(sa, 0, u).astype(jnp.bfloat16)
        prb = gathered(sp, 0, u)
        rhs = jnp.concatenate([jnp.where(low, prb, 0.0), jnp.where(low, 0.0, prb)], axis=0)
        both = jnp.dot(lhs, rhs.astype(jnp.bfloat16), preferred_element_type=jnp.float32)
        both = both.astype(jnp.bfloat16)
        solved[r0 + u] = both
        solved[r0 + 16 + u] = jnp.concatenate([both[:, BLOCK:], both[:, :BLOCK]], axis=1)

    def couple_spread(g, sc, q):
        kp, p = q // 32, q % 32
        r0 = pl.multiple_of(g * 16, 16)
        spread(cpl_v, r0, 2 * ROW * kp, r0, 2 * ROW * kp + ROW, sc, 16 * BLOCK * kp, p)

    def couple(g, sc, up):
        parts = []
        for e in range(2):
            u = up // 4 * 8 + up % 4 + 4 * e
            lhs = [gathered(sc, 16 * BLOCK * kp, u).astype(jnp.bfloat16) for kp in range(kb // 2)]
            rhs = [solved[cols[k, g * 16 + u] ^ (16 * e)] for k in range(kb)]
            parts.append(jnp.dot(jnp.concatenate(lhs, axis=1), jnp.concatenate(rhs, axis=0), preferred_element_type=jnp.float32))
        both = jnp.where(low, parts[0], parts[1]).astype(jnp.bfloat16)
        out_v[2 * g + up // 4, up % 4 * BLOCK : up % 4 * BLOCK + BLOCK, :] = both

    def out_copy(g):
        return pltpu.make_async_copy(out_v.at[pl.ds(2 * g, 2)], out_ref.at[pl.ds(2 * g, 2)], out_sem.at[g])

    def wait(g):
        for copy in interior_copies(g):
            copy.wait()

    def solve_beside(g, sa, sp, na, np_):
        for u in range(16):
            solve(g, sa, sp, u)
            solve_spread(g + 1, na, np_, 2 * u)

    wait(0)
    for p in range(0, BLOCK // 2, 2):
        solve_spread(0, a0, p0, p)

    def two_groups(t, carry):
        wait(2 * t + 1)
        wait(2 * t + 2)
        solve_beside(2 * t, a0, p0, a1, p1)
        solve_beside(2 * t + 1, a1, p1, a0, p0)
        return carry

    lax.fori_loop(0, groups // 2 - 1, two_groups, 0)
    wait(groups - 1)
    for g in range(cgroups):
        coupling_copy(g).wait()
    cols_copy.wait()
    solve_beside(groups - 2, a0, p0, a1, p1)
    for u in range(16):
        solve(groups - 1, a1, p1, u)
        for q in range(8 * u, 8 * u + 8, 2):
            couple_spread(0, c0, q)
    for g in range(cgroups):
        here, there = (c0, c1) if g % 2 == 0 else (c1, c0)
        for up in range(8):
            couple(g, here, up)
            if g + 1 < cgroups:
                for q in range(16 * up, 16 * up + 16, 2):
                    couple_spread(g + 1, there, q)
        out_copy(g).start()
    for g in range(cgroups):
        out_copy(g).wait()


def paired_pieces(block_inverse, probes, coupling, columns, regions):
    nb, ni = block_inverse.shape[0], coupling.shape[0]
    any_place = pl.BlockSpec(memory_space=pl.ANY)
    stage = pltpu.VMEM((16 * BLOCK, 128), jnp.float32)
    big = pltpu.VMEM((64 * BLOCK, 128), jnp.float32)
    return pl.pallas_call(
        pieces_kernel,
        out_shape=jax.ShapeDtypeStruct((regions, ni * BLOCK // regions // 2, 2 * RANK), jnp.bfloat16),
        in_specs=[any_place] * 4,
        out_specs=any_place,
        scratch_shapes=[
            pltpu.SMEM(columns.shape[::-1], jnp.int32),
            pltpu.VMEM(block_inverse.shape, jnp.bfloat16),
            pltpu.VMEM(probes.shape, jnp.bfloat16),
            pltpu.VMEM(coupling.shape, jnp.bfloat16),
            stage, stage, stage, stage, big, big,
            pltpu.VMEM((nb, BLOCK, 128), jnp.bfloat16),
            pltpu.VMEM((regions, ni * BLOCK // regions // 2, 2 * RANK), jnp.bfloat16),
            pltpu.SemaphoreType.DMA((3, nb // 32)),
            pltpu.SemaphoreType.DMA(()),
            pltpu.SemaphoreType.DMA((ni // 16,)),
        ],
        compiler_params=pltpu.CompilerParams(vmem_limit_bytes=58 * MIB),
    )(columns.T, block_inverse, probes, coupling)


def three_parts(x):
    high = x.astype(jnp.bfloat16)
    rest = x - high.astype(jnp.float32)
    middle = rest.astype(jnp.bfloat16)
    low = (rest - middle.astype(jnp.float32)).astype(jnp.bfloat16)
    return jnp.concatenate([high, middle, low], axis=0)


def packed_sums(gram, moment):
    half = gram.shape[0] // 2
    row_at = lax.broadcasted_iota(jnp.int32, (half, half), 0)
    lane_at = lax.broadcasted_iota(jnp.int32, (half, half), 1)
    first, corner, second = gram[:half, :half], gram[:half, half:], gram[half:, half:]
    square = jnp.concatenate([jnp.where(lane_at >= row_at, first, second), corner], axis=1)
    diagonal = jnp.sum(jnp.where(lane_at == row_at, second, 0.0), axis=0, keepdims=True)
    last = jnp.concatenate([moment, diagonal, jnp.zeros_like(diagonal)], axis=1)
    last = jnp.broadcast_to(last, (8, 4 * half))
    return jnp.concatenate([jnp.concatenate([square[: half // 2], square[half // 2 :]], axis=1), last], axis=0)


def unpacked_sums(packed):
    half = packed.shape[1] // 4
    rank = 2 * half
    row_at = lax.broadcasted_iota(jnp.int32, (half, half), 0)
    lane_at = lax.broadcasted_iota(jnp.int32, (half, half), 1)
    square = jnp.concatenate([packed[: half // 2, :rank], packed[: half // 2, rank:]], axis=0)
    turned = jnp.transpose(jnp.concatenate([square, square], axis=1), (1, 0))
    upper, lower = square[:, :half], turned[:half]
    moment, diagonal = packed[half // 2 : half // 2 + 1, :rank], packed[half // 2 : half // 2 + 1, rank : rank + half]
    first = jnp.where(lane_at >= row_at, upper, lower)
    second = jnp.where(lane_at >= row_at, lower, upper)
    second = jnp.where(lane_at == row_at, diagonal, second)
    top = jnp.concatenate([first, square[:, half:]], axis=1)
    return jnp.concatenate([top, jnp.concatenate([turned[half:rank], second], axis=1)], axis=0), moment


def gram_kernel(pairs_ref, res_ref, sums_ref, turned_ref):
    regions, half, lanes = pairs_ref.shape
    rank = lanes // 2
    gram = jnp.zeros((lanes, lanes), jnp.float32)
    moment = jnp.zeros((6, lanes), jnp.float32)
    for r in range(regions):
        pairs = pairs_ref[r]
        at = 2 * r * half
        turned = jnp.transpose(pairs, (1, 0))
        turned_ref[:, at : at + half] = turned[:rank]
        turned_ref[:, at + half : at + 2 * half] = turned[rank:]
        gram += jnp.dot(turned, pairs, preferred_element_type=jnp.float32)
        parts = [three_parts(res_ref[:, at + half * i : at + half * i + half]) for i in range(2)]
        moment += jnp.dot(jnp.concatenate(parts, axis=0), pairs, preferred_element_type=jnp.float32)
    gram = gram[:rank, :rank] + gram[rank:, rank:]
    moment = moment[:3, :rank] + moment[3:, rank:]
    packed = packed_sums(gram, moment[0:1] + moment[1:2] + moment[2:3])
    for s in range(sums_ref.shape[0]):
        sums_ref[s] = packed


def two_parts(x):
    high = x.astype(jnp.bfloat16)
    return jnp.concatenate([high, (x - high.astype(jnp.float32)).astype(jnp.bfloat16)], axis=0)


def inverse_lower(gram):
    rank = gram.shape[0]
    row_at = lax.broadcasted_iota(jnp.int32, (rank, 2 * rank), 0)
    lane_at = lax.broadcasted_iota(jnp.int32, (rank, 2 * rank), 1)
    rest = jnp.concatenate([gram, jnp.zeros_like(gram)], axis=1) + (lane_at == row_at + rank).astype(jnp.float32)
    done = []
    for k in range(0, rank, STEP):
        at = row_at[: rank - k]
        cols = [jnp.broadcast_to(rest[:, k + j : k + j + 1], rest.shape) for j in range(STEP)]
        rows = [rest[j : j + 1, :] for j in range(STEP)]
        pivots = []
        for j in range(STEP):
            pivot = cols[j][j : j + 1, :]
            pivots.append(pivot)
            factor = jnp.where(at > j, cols[j] * (1.0 / pivot), 0.0)
            for l in range(j + 1, STEP):
                cols[l] = cols[l] - factor * cols[l][j : j + 1, :]
                rows[l] = rows[l] - factor[l : l + 1, :] * rows[j]
            rest = rest - factor * rows[j]
        done.append(rest[:STEP, rank:] * lax.rsqrt(jnp.concatenate(pivots, axis=0)[:, :rank]))
        rest = rest[STEP:]
    return jnp.concatenate(done, axis=0)


def finish_kernel(total_rows, sums_ref, rows_ref, basis_ref, corr_ref, basis_v, sem):
    rank, run = rows_ref.shape[0], rows_ref.shape[1] // sem.shape[0]
    regions = sem.shape[0]
    total = sums_ref[0]
    for n in range(1, sums_ref.shape[0]):
        total = total + sums_ref[n]
    gram, moment = unpacked_sums(total)
    lower_inverse = inverse_lower(gram)
    coefficients = jnp.sum(lower_inverse * moment, axis=1, keepdims=True)
    weights = two_parts(lower_inverse * math.sqrt(total_rows))
    shrink = 1.0 / math.sqrt(rank)

    def copy_out(r):
        cols = pl.ds(r * run, run)
        return pltpu.make_async_copy(basis_v.at[:, cols], basis_ref.at[:, cols], sem.at[r])

    for r in range(regions):
        q = jnp.dot(weights, rows_ref[:, r * run : (r + 1) * run], preferred_element_type=jnp.float32)
        q = q[:rank] + q[rank:]
        basis_v[:, r * run : (r + 1) * run] = q
        copy_out(r).start()
        corr_ref[:, r * run : (r + 1) * run] = jnp.sum(q * (coefficients * shrink), axis=0, keepdims=True)
    for r in range(regions):
        copy_out(r).wait()


def per_device(block_inverse, probes, coupling, columns, residual):
    regions, subs = lax.axis_size("region"), lax.axis_size("sub")
    rows_here = residual.shape[0]
    in_vmem = pl.BlockSpec(memory_space=pltpu.VMEM)
    pieces = paired_pieces(block_inverse, probes, coupling, columns, regions)
    owned = lax.all_to_all(pieces, "region", split_axis=0, concat_axis=0, tiled=True)
    sums, turned = pl.pallas_call(
        gram_kernel,
        out_shape=(
            jax.ShapeDtypeStruct((subs, RANK // 4 + 8, 2 * RANK), jnp.float32),
            jax.ShapeDtypeStruct((RANK, rows_here), jnp.bfloat16),
        ),
        in_specs=[in_vmem, in_vmem],
        out_specs=(in_vmem, in_vmem),
        compiler_params=pltpu.CompilerParams(vmem_limit_bytes=16 * MIB),
    )(owned, residual.reshape(1, rows_here))
    sums = lax.all_to_all(sums, "sub", split_axis=0, concat_axis=0, tiled=True)
    basis_t, correction = pl.pallas_call(
        functools.partial(finish_kernel, rows_here * subs),
        out_shape=(
            jax.ShapeDtypeStruct((RANK, rows_here), jnp.float32),
            jax.ShapeDtypeStruct((1, rows_here), jnp.float32),
        ),
        in_specs=[in_vmem, in_vmem],
        out_specs=(pl.BlockSpec(memory_space=pl.ANY), in_vmem),
        scratch_shapes=[pltpu.VMEM((RANK, rows_here), jnp.float32), pltpu.SemaphoreType.DMA((regions,))],
        compiler_params=pltpu.CompilerParams(vmem_limit_bytes=16 * MIB),
    )(sums, turned)
    return basis_t.T, correction.reshape(rows_here)


def solution(mesh):
    blocks = P(("region", "sub"), None)
    rows = P(("region", "sub"))
    return jax.shard_map(
        per_device,
        mesh=mesh,
        in_specs=(blocks, blocks, blocks, blocks, rows),
        out_specs=(blocks, rows),
        check_vma=False,
    )
```

```python
import functools
import math

import jax
import jax.numpy as jnp
from jax import lax
from jax.experimental import pallas as pl
from jax.experimental.pallas import tpu as pltpu
from jax.sharding import PartitionSpec as P

BLOCK = 64
RANK = 64
ROW = BLOCK * BLOCK
MIB = 2**20
STEP = 16


def spread(src, r0, c0, r1, c1, dst, base, p):
    x = src[pl.ds(r0, 16), pl.ds(c0 + 128 * p, 256)]
    y = src[pl.ds(r1, 16), pl.ds(c1 + 128 * p, 256)]
    x = [x[:, BLOCK * i : BLOCK * i + BLOCK] for i in range(4)]
    y = [y[:, BLOCK * i : BLOCK * i + BLOCK] for i in range(4)]
    even = jnp.concatenate([x[0], y[0], x[2], y[2]], axis=1).astype(jnp.float32)
    odd = jnp.concatenate([x[1], y[1], x[3], y[3]], axis=1).astype(jnp.float32)
    for h in range(2):
        for q in range(2):
            at = base + 8 * BLOCK * h + 16 * (p + q)
            dst[pl.ds(at, 8), :] = even[8 * h : 8 * h + 8, 128 * q : 128 * q + 128]
            dst[pl.ds(at + 8, 8), :] = odd[8 * h : 8 * h + 8, 128 * q : 128 * q + 128]


def gathered(stage, base, u):
    return stage[pl.ds(base + u // 8 * 8 * BLOCK + u % 8, BLOCK, stride=8), :]


def pieces_kernel(cols_hbm, inv_ref, prb_ref, cpl_ref, out_ref, cols, inv_v, prb_v, cpl_v, a0, a1, p0, p1, c0, c1, solved, out_v, sem, cols_sem, out_sem):
    nb, ni = inv_ref.shape[0], cpl_ref.shape[0]
    kb = cpl_ref.shape[1] // ROW
    groups, cgroups = nb // 32, ni // 16

    def interior_copies(g):
        rows = pl.ds(pl.multiple_of(g * 32, 32), 32)
        return (
            pltpu.make_async_copy(inv_ref.at[rows], inv_v.at[rows], sem.at[0, g]),
            pltpu.make_async_copy(prb_ref.at[rows], prb_v.at[rows], sem.at[1, g]),
        )

    def coupling_copy(g):
        rows = pl.ds(pl.multiple_of(g * 16, 16), 16)
        return pltpu.make_async_copy(cpl_ref.at[rows], cpl_v.at[rows], sem.at[2, g])

    cols_copy = pltpu.make_async_copy(cols_hbm, cols, cols_sem)
    for copy in interior_copies(0):
        copy.start()
    cols_copy.start()
    for g in range(1, groups):
        for copy in interior_copies(g):
            copy.start()
    for g in range(cgroups):
        coupling_copy(g).start()
    low = lax.broadcasted_iota(jnp.int32, (BLOCK, 128), 1) < BLOCK

    def solve_spread(g, sa, sp, p):
        r0 = pl.multiple_of(g * 32, 32)
        spread(inv_v, r0, 0, r0 + 16, 0, sa, 0, p)
        spread(prb_v, r0, 0, r0 + 16, 0, sp, 0, p)

    def solve(g, sa, sp, u):
        r0 = g * 32
        lhs = gathered(sa, 0, u).astype(jnp.bfloat16)
        prb = gathered(sp, 0, u)
        rhs = jnp.concatenate([jnp.where(low, prb, 0.0), jnp.where(low, 0.0, prb)], axis=0)
        both = jnp.dot(lhs, rhs.astype(jnp.bfloat16), preferred_element_type=jnp.float32)
        both = both.astype(jnp.bfloat16)
        solved[r0 + u] = both
        solved[r0 + 16 + u] = jnp.concatenate([both[:, BLOCK:], both[:, :BLOCK]], axis=1)

    def couple_spread(g, sc, q):
        kp, p = q // 32, q % 32
        r0 = pl.multiple_of(g * 16, 16)
        spread(cpl_v, r0, 2 * ROW * kp, r0, 2 * ROW * kp + ROW, sc, 16 * BLOCK * kp, p)

    def couple(g, sc, up):
        parts = []
        for e in range(2):
            u = up // 4 * 8 + up % 4 + 4 * e
            lhs = [gathered(sc, 16 * BLOCK * kp, u).astype(jnp.bfloat16) for kp in range(kb // 2)]
            rhs = [solved[cols[k, g * 16 + u] ^ (16 * e)] for k in range(kb)]
            parts.append(jnp.dot(jnp.concatenate(lhs, axis=1), jnp.concatenate(rhs, axis=0), preferred_element_type=jnp.float32))
        both = jnp.where(low, parts[0], parts[1]).astype(jnp.bfloat16)
        out_v[2 * g + up // 4, up % 4 * BLOCK : up % 4 * BLOCK + BLOCK, :] = both

    def out_copy(g):
        return pltpu.make_async_copy(out_v.at[pl.ds(2 * g, 2)], out_ref.at[pl.ds(2 * g, 2)], out_sem.at[g])

    def wait(g):
        for copy in interior_copies(g):
            copy.wait()

    def solve_beside(g, sa, sp, na, np_):
        for u in range(16):
            solve(g, sa, sp, u)
            solve_spread(g + 1, na, np_, 2 * u)

    wait(0)
    for p in range(0, BLOCK // 2, 2):
        solve_spread(0, a0, p0, p)

    def two_groups(t, carry):
        wait(2 * t + 1)
        wait(2 * t + 2)
        solve_beside(2 * t, a0, p0, a1, p1)
        solve_beside(2 * t + 1, a1, p1, a0, p0)
        return carry

    lax.fori_loop(0, groups // 2 - 1, two_groups, 0)
    wait(groups - 1)
    for g in range(cgroups):
        coupling_copy(g).wait()
    cols_copy.wait()
    solve_beside(groups - 2, a0, p0, a1, p1)
    for u in range(16):
        solve(groups - 1, a1, p1, u)
        for q in range(8 * u, 8 * u + 8, 2):
            couple_spread(0, c0, q)
    for g in range(cgroups):
        here, there = (c0, c1) if g % 2 == 0 else (c1, c0)
        for up in range(8):
            couple(g, here, up)
            if g + 1 < cgroups:
                for q in range(16 * up, 16 * up + 16, 2):
                    couple_spread(g + 1, there, q)
        out_copy(g).start()
    for g in range(cgroups):
        out_copy(g).wait()


def paired_pieces(block_inverse, probes, coupling, columns, regions):
    nb, ni = block_inverse.shape[0], coupling.shape[0]
    any_place = pl.BlockSpec(memory_space=pl.ANY)
    stage = pltpu.VMEM((16 * BLOCK, 128), jnp.float32)
    big = pltpu.VMEM((64 * BLOCK, 128), jnp.float32)
    return pl.pallas_call(
        pieces_kernel,
        out_shape=jax.ShapeDtypeStruct((regions, ni * BLOCK // regions // 2, 2 * RANK), jnp.bfloat16),
        in_specs=[any_place] * 4,
        out_specs=any_place,
        scratch_shapes=[
            pltpu.SMEM(columns.shape[::-1], jnp.int32),
            pltpu.VMEM(block_inverse.shape, jnp.bfloat16),
            pltpu.VMEM(probes.shape, jnp.bfloat16),
            pltpu.VMEM(coupling.shape, jnp.bfloat16),
            stage, stage, stage, stage, big, big,
            pltpu.VMEM((nb, BLOCK, 128), jnp.bfloat16),
            pltpu.VMEM((regions, ni * BLOCK // regions // 2, 2 * RANK), jnp.bfloat16),
            pltpu.SemaphoreType.DMA((3, nb // 32)),
            pltpu.SemaphoreType.DMA(()),
            pltpu.SemaphoreType.DMA((ni // 16,)),
        ],
        compiler_params=pltpu.CompilerParams(vmem_limit_bytes=58 * MIB),
    )(columns.T, block_inverse, probes, coupling)


def three_parts(x):
    high = x.astype(jnp.bfloat16)
    rest = x - high.astype(jnp.float32)
    middle = rest.astype(jnp.bfloat16)
    low = (rest - middle.astype(jnp.float32)).astype(jnp.bfloat16)
    return jnp.concatenate([high, middle, low], axis=0)


def packed_sums(gram, moment):
    half = gram.shape[0] // 2
    row_at = lax.broadcasted_iota(jnp.int32, (half, half), 0)
    lane_at = lax.broadcasted_iota(jnp.int32, (half, half), 1)
    first, corner, second = gram[:half, :half], gram[:half, half:], gram[half:, half:]
    square = jnp.concatenate([jnp.where(lane_at >= row_at, first, second), corner], axis=1)
    diagonal = jnp.sum(jnp.where(lane_at == row_at, second, 0.0), axis=0, keepdims=True)
    last = jnp.concatenate([moment, diagonal, jnp.zeros_like(diagonal)], axis=1)
    square = jnp.concatenate([square[: half // 2], square[half // 2 :]], axis=1)
    return [square[i : i + 1] for i in range(half // 2)] + [last]


def unpacked_sums(packed):
    lanes = 2 * RANK
    packed = jnp.concatenate([packed[:, i : i + lanes] for i in range(0, packed.shape[1], lanes)], axis=0)
    half = lanes // 4
    rank = 2 * half
    row_at = lax.broadcasted_iota(jnp.int32, (half, half), 0)
    lane_at = lax.broadcasted_iota(jnp.int32, (half, half), 1)
    square = jnp.concatenate([packed[: half // 2, :rank], packed[: half // 2, rank:]], axis=0)
    turned = jnp.transpose(jnp.concatenate([square, square], axis=1), (1, 0))
    upper, lower = square[:, :half], turned[:half]
    moment, diagonal = packed[half // 2 : half // 2 + 1, :rank], packed[half // 2 : half // 2 + 1, rank : rank + half]
    first = jnp.where(lane_at >= row_at, upper, lower)
    second = jnp.where(lane_at >= row_at, lower, upper)
    second = jnp.where(lane_at == row_at, diagonal, second)
    top = jnp.concatenate([first, square[:, half:]], axis=1)
    return jnp.concatenate([top, jnp.concatenate([turned[half:rank], second], axis=1)], axis=0), moment


def gram_kernel(pairs_ref, res_ref, sums_ref, turned_ref):
    regions, half, lanes = pairs_ref.shape
    rank = lanes // 2
    gram = jnp.zeros((lanes, lanes), jnp.float32)
    moment = jnp.zeros((6, lanes), jnp.float32)
    for r in range(regions):
        pairs = pairs_ref[r]
        at = 2 * r * half
        turned = jnp.transpose(pairs, (1, 0))
        turned_ref[:, at : at + half] = turned[:rank]
        turned_ref[:, at + half : at + 2 * half] = turned[rank:]
        gram += jnp.dot(turned, pairs, preferred_element_type=jnp.float32)
        parts = [three_parts(res_ref[:, at + half * i : at + half * i + half]) for i in range(2)]
        moment += jnp.dot(jnp.concatenate(parts, axis=0), pairs, preferred_element_type=jnp.float32)
    gram = gram[:rank, :rank] + gram[rank:, rank:]
    moment = moment[:3, :rank] + moment[3:, rank:]
    packed = packed_sums(gram, moment[0:1] + moment[1:2] + moment[2:3])
    for i, row in enumerate(packed):
        for s in range(sums_ref.shape[0]):
            sums_ref[s, :, lanes * i : lanes * i + lanes] = row


def two_parts(x):
    high = x.astype(jnp.bfloat16)
    return jnp.concatenate([high, (x - high.astype(jnp.float32)).astype(jnp.bfloat16)], axis=0)


def inverse_lower(gram):
    rank = gram.shape[0]
    row_at = lax.broadcasted_iota(jnp.int32, (rank, 2 * rank), 0)
    lane_at = lax.broadcasted_iota(jnp.int32, (rank, 2 * rank), 1)
    rest = jnp.concatenate([gram, jnp.zeros_like(gram)], axis=1) + (lane_at == row_at + rank).astype(jnp.float32)
    done = []
    for k in range(0, rank, STEP):
        at = row_at[: rank - k]
        cols = [jnp.broadcast_to(rest[:, k + j : k + j + 1], rest.shape) for j in range(STEP)]
        rows = [rest[j : j + 1, :] for j in range(STEP)]
        pivots = []
        for j in range(STEP):
            pivot = cols[j][j : j + 1, :]
            pivots.append(pivot)
            factor = jnp.where(at > j, cols[j] * (1.0 / pivot), 0.0)
            for l in range(j + 1, STEP):
                cols[l] = cols[l] - factor * cols[l][j : j + 1, :]
                rows[l] = rows[l] - factor[l : l + 1, :] * rows[j]
            rest = rest - factor * rows[j]
        done.append(rest[:STEP, rank:] * lax.rsqrt(jnp.concatenate(pivots, axis=0)[:, :rank]))
        rest = rest[STEP:]
    return jnp.concatenate(done, axis=0)


def finish_kernel(total_rows, sums_ref, rows_ref, basis_ref, corr_ref, basis_v, sem):
    rank, run = rows_ref.shape[0], rows_ref.shape[1] // sem.shape[0]
    regions = sem.shape[0]
    total = sums_ref[0]
    for n in range(1, sums_ref.shape[0]):
        total = total + sums_ref[n]
    gram, moment = unpacked_sums(total)
    lower_inverse = inverse_lower(gram)
    coefficients = jnp.sum(lower_inverse * moment, axis=1, keepdims=True)
    weights = two_parts(lower_inverse * math.sqrt(total_rows))
    shrink = 1.0 / math.sqrt(rank)

    def copy_out(r):
        cols = pl.ds(r * run, run)
        return pltpu.make_async_copy(basis_v.at[:, cols], basis_ref.at[:, cols], sem.at[r])

    for r in range(regions):
        q = jnp.dot(weights, rows_ref[:, r * run : (r + 1) * run], preferred_element_type=jnp.float32)
        q = q[:rank] + q[rank:]
        basis_v[:, r * run : (r + 1) * run] = q
        copy_out(r).start()
        corr_ref[:, r * run : (r + 1) * run] = jnp.sum(q * (coefficients * shrink), axis=0, keepdims=True)
    for r in range(regions):
        copy_out(r).wait()


def per_device(block_inverse, probes, coupling, columns, residual):
    regions, subs = lax.axis_size("region"), lax.axis_size("sub")
    rows_here = residual.shape[0]
    in_vmem = pl.BlockSpec(memory_space=pltpu.VMEM)
    pieces = paired_pieces(block_inverse, probes, coupling, columns, regions)
    owned = lax.all_to_all(pieces, "region", split_axis=0, concat_axis=0, tiled=True)
    sums, turned = pl.pallas_call(
        gram_kernel,
        out_shape=(
            jax.ShapeDtypeStruct((subs, 1, (RANK // 4 + 1) * 2 * RANK), jnp.float32),
            jax.ShapeDtypeStruct((RANK, rows_here), jnp.bfloat16),
        ),
        in_specs=[in_vmem, in_vmem],
        out_specs=(in_vmem, in_vmem),
        compiler_params=pltpu.CompilerParams(vmem_limit_bytes=16 * MIB),
    )(owned, residual.reshape(1, rows_here))
    sums = lax.all_to_all(sums, "sub", split_axis=0, concat_axis=0, tiled=True)
    basis_t, correction = pl.pallas_call(
        functools.partial(finish_kernel, rows_here * subs),
        out_shape=(
            jax.ShapeDtypeStruct((RANK, rows_here), jnp.float32),
            jax.ShapeDtypeStruct((1, rows_here), jnp.float32),
        ),
        in_specs=[in_vmem, in_vmem],
        out_specs=(pl.BlockSpec(memory_space=pl.ANY), in_vmem),
        scratch_shapes=[pltpu.VMEM((RANK, rows_here), jnp.float32), pltpu.SemaphoreType.DMA((regions,))],
        compiler_params=pltpu.CompilerParams(vmem_limit_bytes=16 * MIB),
    )(sums, turned)
    return basis_t.T, correction.reshape(rows_here)


def solution(mesh):
    blocks = P(("region", "sub"), None)
    rows = P(("region", "sub"))
    return jax.shard_map(
        per_device,
        mesh=mesh,
        in_specs=(blocks, blocks, blocks, blocks, rows),
        out_specs=(blocks, rows),
        check_vma=False,
    )
```

```python
import functools
import math

import jax
import jax.numpy as jnp
from jax import lax
from jax.experimental import pallas as pl
from jax.experimental.pallas import tpu as pltpu
from jax.sharding import PartitionSpec as P

BLOCK = 64
RANK = 64
ROW = BLOCK * BLOCK
MIB = 2**20
STEP = 16
SUB_Y = 4


def spread(src, r0, c0, r1, c1, dst, base, p):
    x = src[pl.ds(r0, 16), pl.ds(c0 + 128 * p, 256)]
    y = src[pl.ds(r1, 16), pl.ds(c1 + 128 * p, 256)]
    x = [x[:, BLOCK * i : BLOCK * i + BLOCK] for i in range(4)]
    y = [y[:, BLOCK * i : BLOCK * i + BLOCK] for i in range(4)]
    even = jnp.concatenate([x[0], y[0], x[2], y[2]], axis=1).astype(jnp.float32)
    odd = jnp.concatenate([x[1], y[1], x[3], y[3]], axis=1).astype(jnp.float32)
    for h in range(2):
        for q in range(2):
            at = base + 8 * BLOCK * h + 16 * (p + q)
            dst[pl.ds(at, 8), :] = even[8 * h : 8 * h + 8, 128 * q : 128 * q + 128]
            dst[pl.ds(at + 8, 8), :] = odd[8 * h : 8 * h + 8, 128 * q : 128 * q + 128]


def gathered(stage, base, u):
    return stage[pl.ds(base + u // 8 * 8 * BLOCK + u % 8, BLOCK, stride=8), :]


def pieces_kernel(cols_hbm, inv_ref, prb_ref, cpl_ref, out_ref, cols, inv_v, prb_v, cpl_v, a0, a1, p0, p1, c0, c1, solved, out_v, sem, cols_sem, out_sem):
    nb, ni = inv_ref.shape[0], cpl_ref.shape[0]
    kb = cpl_ref.shape[1] // ROW
    groups, cgroups = nb // 32, ni // 16

    def interior_copies(g):
        rows = pl.ds(pl.multiple_of(g * 32, 32), 32)
        return (
            pltpu.make_async_copy(inv_ref.at[rows], inv_v.at[rows], sem.at[0, g]),
            pltpu.make_async_copy(prb_ref.at[rows], prb_v.at[rows], sem.at[1, g]),
        )

    def coupling_copy(g):
        rows = pl.ds(pl.multiple_of(g * 16, 16), 16)
        return pltpu.make_async_copy(cpl_ref.at[rows], cpl_v.at[rows], sem.at[2, g])

    cols_copy = pltpu.make_async_copy(cols_hbm, cols, cols_sem)
    for copy in interior_copies(0):
        copy.start()
    cols_copy.start()
    for g in range(1, groups):
        for copy in interior_copies(g):
            copy.start()
    for g in range(cgroups):
        coupling_copy(g).start()
    low = lax.broadcasted_iota(jnp.int32, (BLOCK, 128), 1) < BLOCK

    def solve_spread(g, sa, sp, p):
        r0 = pl.multiple_of(g * 32, 32)
        spread(inv_v, r0, 0, r0 + 16, 0, sa, 0, p)
        spread(prb_v, r0, 0, r0 + 16, 0, sp, 0, p)

    def solve(g, sa, sp, u):
        r0 = g * 32
        lhs = gathered(sa, 0, u).astype(jnp.bfloat16)
        prb = gathered(sp, 0, u)
        rhs = jnp.concatenate([jnp.where(low, prb, 0.0), jnp.where(low, 0.0, prb)], axis=0)
        both = jnp.dot(lhs, rhs.astype(jnp.bfloat16), preferred_element_type=jnp.float32)
        both = both.astype(jnp.bfloat16)
        solved[r0 + u] = both
        solved[r0 + 16 + u] = jnp.concatenate([both[:, BLOCK:], both[:, :BLOCK]], axis=1)

    def couple_spread(g, sc, q):
        kp, p = q // 32, q % 32
        r0 = pl.multiple_of(g * 16, 16)
        spread(cpl_v, r0, 2 * ROW * kp, r0, 2 * ROW * kp + ROW, sc, 16 * BLOCK * kp, p)

    def couple(g, sc, up):
        parts = []
        for e in range(2):
            u = up // 4 * 8 + up % 4 + 4 * e
            lhs = [gathered(sc, 16 * BLOCK * kp, u).astype(jnp.bfloat16) for kp in range(kb // 2)]
            rhs = [solved[cols[k, g * 16 + u] ^ (16 * e)] for k in range(kb)]
            parts.append(jnp.dot(jnp.concatenate(lhs, axis=1), jnp.concatenate(rhs, axis=0), preferred_element_type=jnp.float32))
        both = jnp.where(low, parts[0], parts[1]).astype(jnp.bfloat16)
        out_v[2 * g + up // 4, up % 4 * BLOCK : up % 4 * BLOCK + BLOCK, :] = both

    def out_copy(g):
        return pltpu.make_async_copy(out_v.at[pl.ds(2 * g, 2)], out_ref.at[pl.ds(2 * g, 2)], out_sem.at[g])

    def wait(g):
        for copy in interior_copies(g):
            copy.wait()

    def solve_beside(g, sa, sp, na, np_):
        for u in range(16):
            solve(g, sa, sp, u)
            solve_spread(g + 1, na, np_, 2 * u)

    wait(0)
    for p in range(0, BLOCK // 2, 2):
        solve_spread(0, a0, p0, p)

    def two_groups(t, carry):
        wait(2 * t + 1)
        wait(2 * t + 2)
        solve_beside(2 * t, a0, p0, a1, p1)
        solve_beside(2 * t + 1, a1, p1, a0, p0)
        return carry

    lax.fori_loop(0, groups // 2 - 1, two_groups, 0)
    wait(groups - 1)
    for g in range(cgroups):
        coupling_copy(g).wait()
    cols_copy.wait()
    solve_beside(groups - 2, a0, p0, a1, p1)
    for u in range(16):
        solve(groups - 1, a1, p1, u)
        for q in range(8 * u, 8 * u + 8, 2):
            couple_spread(0, c0, q)
    for g in range(cgroups):
        here, there = (c0, c1) if g % 2 == 0 else (c1, c0)
        for up in range(8):
            couple(g, here, up)
            if g + 1 < cgroups:
                for q in range(16 * up, 16 * up + 16, 2):
                    couple_spread(g + 1, there, q)
        out_copy(g).start()
    for g in range(cgroups):
        out_copy(g).wait()


def paired_pieces(block_inverse, probes, coupling, columns, regions):
    nb, ni = block_inverse.shape[0], coupling.shape[0]
    any_place = pl.BlockSpec(memory_space=pl.ANY)
    stage = pltpu.VMEM((16 * BLOCK, 128), jnp.float32)
    big = pltpu.VMEM((64 * BLOCK, 128), jnp.float32)
    return pl.pallas_call(
        pieces_kernel,
        out_shape=jax.ShapeDtypeStruct((regions, ni * BLOCK // regions // 2, 2 * RANK), jnp.bfloat16),
        in_specs=[any_place] * 4,
        out_specs=any_place,
        scratch_shapes=[
            pltpu.SMEM(columns.shape[::-1], jnp.int32),
            pltpu.VMEM(block_inverse.shape, jnp.bfloat16),
            pltpu.VMEM(probes.shape, jnp.bfloat16),
            pltpu.VMEM(coupling.shape, jnp.bfloat16),
            stage, stage, stage, stage, big, big,
            pltpu.VMEM((nb, BLOCK, 128), jnp.bfloat16),
            pltpu.VMEM((regions, ni * BLOCK // regions // 2, 2 * RANK), jnp.bfloat16),
            pltpu.SemaphoreType.DMA((3, nb // 32)),
            pltpu.SemaphoreType.DMA(()),
            pltpu.SemaphoreType.DMA((ni // 16,)),
        ],
        compiler_params=pltpu.CompilerParams(vmem_limit_bytes=58 * MIB),
    )(columns.T, block_inverse, probes, coupling)


def three_parts(x):
    high = x.astype(jnp.bfloat16)
    rest = x - high.astype(jnp.float32)
    middle = rest.astype(jnp.bfloat16)
    low = (rest - middle.astype(jnp.float32)).astype(jnp.bfloat16)
    return jnp.concatenate([high, middle, low], axis=0)


def packed_sums(gram, moment):
    half = gram.shape[0] // 2
    row_at = lax.broadcasted_iota(jnp.int32, (half, half), 0)
    lane_at = lax.broadcasted_iota(jnp.int32, (half, half), 1)
    first, corner, second = gram[:half, :half], gram[:half, half:], gram[half:, half:]
    square = jnp.concatenate([jnp.where(lane_at >= row_at, first, second), corner], axis=1)
    diagonal = jnp.sum(jnp.where(lane_at == row_at, second, 0.0), axis=0, keepdims=True)
    last = jnp.concatenate([moment, diagonal, jnp.zeros_like(diagonal)], axis=1)
    square = jnp.concatenate([square[: half // 2], square[half // 2 :]], axis=1)
    return [square[i : i + 1] for i in range(half // 2)] + [last]


def unpacked_sums(packed):
    lanes = 2 * RANK
    packed = jnp.concatenate([packed[:, i : i + lanes] for i in range(0, packed.shape[1], lanes)], axis=0)
    half = lanes // 4
    rank = 2 * half
    row_at = lax.broadcasted_iota(jnp.int32, (half, half), 0)
    lane_at = lax.broadcasted_iota(jnp.int32, (half, half), 1)
    square = jnp.concatenate([packed[: half // 2, :rank], packed[: half // 2, rank:]], axis=0)
    turned = jnp.transpose(jnp.concatenate([square, square], axis=1), (1, 0))
    upper, lower = square[:, :half], turned[:half]
    moment, diagonal = packed[half // 2 : half // 2 + 1, :rank], packed[half // 2 : half // 2 + 1, rank : rank + half]
    first = jnp.where(lane_at >= row_at, upper, lower)
    second = jnp.where(lane_at >= row_at, lower, upper)
    second = jnp.where(lane_at == row_at, diagonal, second)
    top = jnp.concatenate([first, square[:, half:]], axis=1)
    return jnp.concatenate([top, jnp.concatenate([turned[half:rank], second], axis=1)], axis=0), moment


def gram_kernel(pairs_ref, res_ref, sums_ref, turned_ref):
    regions, half, lanes = pairs_ref.shape
    rank = lanes // 2
    gram = jnp.zeros((lanes, lanes), jnp.float32)
    moment = jnp.zeros((6, lanes), jnp.float32)
    for r in range(regions):
        pairs = pairs_ref[r]
        at = 2 * r * half
        turned = jnp.transpose(pairs, (1, 0))
        turned_ref[:, at : at + half] = turned[:rank]
        turned_ref[:, at + half : at + 2 * half] = turned[rank:]
        gram += jnp.dot(turned, pairs, preferred_element_type=jnp.float32)
        parts = [three_parts(res_ref[:, at + half * i : at + half * i + half]) for i in range(2)]
        moment += jnp.dot(jnp.concatenate(parts, axis=0), pairs, preferred_element_type=jnp.float32)
    gram = gram[:rank, :rank] + gram[rank:, rank:]
    moment = moment[:3, :rank] + moment[3:, rank:]
    packed = packed_sums(gram, moment[0:1] + moment[1:2] + moment[2:3])
    for i, row in enumerate(packed):
        sums_ref[0, :, lanes * i : lanes * i + lanes] = row


def two_parts(x):
    high = x.astype(jnp.bfloat16)
    return jnp.concatenate([high, (x - high.astype(jnp.float32)).astype(jnp.bfloat16)], axis=0)


def inverse_lower(gram):
    rank = gram.shape[0]
    row_at = lax.broadcasted_iota(jnp.int32, (rank, 2 * rank), 0)
    lane_at = lax.broadcasted_iota(jnp.int32, (rank, 2 * rank), 1)
    rest = jnp.concatenate([gram, jnp.zeros_like(gram)], axis=1) + (lane_at == row_at + rank).astype(jnp.float32)
    done = []
    for k in range(0, rank, STEP):
        at = row_at[: rank - k]
        cols = [jnp.broadcast_to(rest[:, k + j : k + j + 1], rest.shape) for j in range(STEP)]
        rows = [rest[j : j + 1, :] for j in range(STEP)]
        pivots = []
        for j in range(STEP):
            pivot = cols[j][j : j + 1, :]
            pivots.append(pivot)
            factor = jnp.where(at > j, cols[j] * (1.0 / pivot), 0.0)
            for l in range(j + 1, STEP):
                cols[l] = cols[l] - factor * cols[l][j : j + 1, :]
                rows[l] = rows[l] - factor[l : l + 1, :] * rows[j]
            rest = rest - factor * rows[j]
        done.append(rest[:STEP, rank:] * lax.rsqrt(jnp.concatenate(pivots, axis=0)[:, :rank]))
        rest = rest[STEP:]
    return jnp.concatenate(done, axis=0)


def finish_kernel(total_rows, sums_ref, rows_ref, basis_ref, corr_ref, basis_v, sem):
    rank, run = rows_ref.shape[0], rows_ref.shape[1] // sem.shape[0]
    regions = sem.shape[0]
    total = sums_ref[0]
    for n in range(1, sums_ref.shape[0]):
        total = total + sums_ref[n]
    gram, moment = unpacked_sums(total)
    lower_inverse = inverse_lower(gram)
    coefficients = jnp.sum(lower_inverse * moment, axis=1, keepdims=True)
    weights = two_parts(lower_inverse * math.sqrt(total_rows))
    shrink = 1.0 / math.sqrt(rank)

    def copy_out(r):
        cols = pl.ds(r * run, run)
        return pltpu.make_async_copy(basis_v.at[:, cols], basis_ref.at[:, cols], sem.at[r])

    for r in range(regions):
        q = jnp.dot(weights, rows_ref[:, r * run : (r + 1) * run], preferred_element_type=jnp.float32)
        q = q[:rank] + q[rank:]
        basis_v[:, r * run : (r + 1) * run] = q
        copy_out(r).start()
        corr_ref[:, r * run : (r + 1) * run] = jnp.sum(q * (coefficients * shrink), axis=0, keepdims=True)
    for r in range(regions):
        copy_out(r).wait()


def per_device(block_inverse, probes, coupling, columns, residual):
    regions, subs = lax.axis_size("region"), lax.axis_size("sub")
    rows_here = residual.shape[0]
    in_vmem = pl.BlockSpec(memory_space=pltpu.VMEM)
    pieces = paired_pieces(block_inverse, probes, coupling, columns, regions)
    owned = lax.all_to_all(pieces, "region", split_axis=0, concat_axis=0, tiled=True)
    sums, turned = pl.pallas_call(
        gram_kernel,
        out_shape=(
            jax.ShapeDtypeStruct((1, 1, (RANK // 4 + 1) * 2 * RANK), jnp.float32),
            jax.ShapeDtypeStruct((RANK, rows_here), jnp.bfloat16),
        ),
        in_specs=[in_vmem, in_vmem],
        out_specs=(in_vmem, in_vmem),
        compiler_params=pltpu.CompilerParams(vmem_limit_bytes=16 * MIB),
    )(owned, residual.reshape(1, rows_here))
    near = subs // SUB_Y
    sums = sums + lax.ppermute(sums, "sub", [(i, i ^ near) for i in range(subs)])
    outer = [i for i in range(subs) if i // near % 4 in (0, 3)]
    inner = [i for i in range(subs) if i // near % 4 in (1, 2)]
    sums = jnp.broadcast_to(sums, (subs // 2,) + sums.shape[1:])
    sums = lax.all_to_all(sums, "sub", split_axis=0, concat_axis=0, tiled=True, axis_index_groups=[outer, inner])
    basis_t, correction = pl.pallas_call(
        functools.partial(finish_kernel, rows_here * subs),
        out_shape=(
            jax.ShapeDtypeStruct((RANK, rows_here), jnp.float32),
            jax.ShapeDtypeStruct((1, rows_here), jnp.float32),
        ),
        in_specs=[in_vmem, in_vmem],
        out_specs=(pl.BlockSpec(memory_space=pl.ANY), in_vmem),
        scratch_shapes=[pltpu.VMEM((RANK, rows_here), jnp.float32), pltpu.SemaphoreType.DMA((regions,))],
        compiler_params=pltpu.CompilerParams(vmem_limit_bytes=16 * MIB),
    )(sums, turned)
    return basis_t.T, correction.reshape(rows_here)


def solution(mesh):
    blocks = P(("region", "sub"), None)
    rows = P(("region", "sub"))
    return jax.shard_map(
        per_device,
        mesh=mesh,
        in_specs=(blocks, blocks, blocks, blocks, rows),
        out_specs=(blocks, rows),
        check_vma=False,
    )
```

```python
import functools
import math

import jax
import jax.numpy as jnp
from jax import lax
from jax.experimental import pallas as pl
from jax.experimental.pallas import tpu as pltpu
from jax.sharding import PartitionSpec as P

BLOCK = 64
RANK = 64
ROW = BLOCK * BLOCK
MIB = 2**20
STEP = 16
SUB_Y = 4


def spread(src, r0, c0, r1, c1, dst, base, p):
    x = src[pl.ds(r0, 16), pl.ds(c0 + 128 * p, 256)]
    y = src[pl.ds(r1, 16), pl.ds(c1 + 128 * p, 256)]
    x = [x[:, BLOCK * i : BLOCK * i + BLOCK] for i in range(4)]
    y = [y[:, BLOCK * i : BLOCK * i + BLOCK] for i in range(4)]
    even = jnp.concatenate([x[0], y[0], x[2], y[2]], axis=1).astype(jnp.float32)
    odd = jnp.concatenate([x[1], y[1], x[3], y[3]], axis=1).astype(jnp.float32)
    for h in range(2):
        for q in range(2):
            at = base + 8 * BLOCK * h + 16 * (p + q)
            dst[pl.ds(at, 8), :] = even[8 * h : 8 * h + 8, 128 * q : 128 * q + 128]
            dst[pl.ds(at + 8, 8), :] = odd[8 * h : 8 * h + 8, 128 * q : 128 * q + 128]


def gathered(stage, base, u):
    return stage[pl.ds(base + u // 8 * 8 * BLOCK + u % 8, BLOCK, stride=8), :]


def pieces_kernel(cols_hbm, inv_ref, prb_ref, cpl_ref, out_ref, cols, inv_v, prb_v, cpl_v, a0, a1, p0, p1, c0, c1, solved, out_v, sem, cols_sem, out_sem):
    nb, ni = inv_ref.shape[0], cpl_ref.shape[0]
    kb = cpl_ref.shape[1] // ROW
    groups, cgroups = nb // 32, ni // 16

    def interior_copies(g):
        rows = pl.ds(pl.multiple_of(g * 32, 32), 32)
        return (
            pltpu.make_async_copy(inv_ref.at[rows], inv_v.at[rows], sem.at[0, g]),
            pltpu.make_async_copy(prb_ref.at[rows], prb_v.at[rows], sem.at[1, g]),
        )

    def coupling_copy(g):
        rows = pl.ds(pl.multiple_of(g * 16, 16), 16)
        return pltpu.make_async_copy(cpl_ref.at[rows], cpl_v.at[rows], sem.at[2, g])

    cols_copy = pltpu.make_async_copy(cols_hbm, cols, cols_sem)
    for copy in interior_copies(0):
        copy.start()
    cols_copy.start()
    for g in range(1, groups):
        for copy in interior_copies(g):
            copy.start()
    for g in range(cgroups):
        coupling_copy(g).start()
    low = lax.broadcasted_iota(jnp.int32, (BLOCK, 128), 1) < BLOCK

    def solve_spread(g, sa, sp, p):
        r0 = pl.multiple_of(g * 32, 32)
        spread(inv_v, r0, 0, r0 + 16, 0, sa, 0, p)
        spread(prb_v, r0, 0, r0 + 16, 0, sp, 0, p)

    def solve(g, sa, sp, u):
        r0 = g * 32
        lhs = gathered(sa, 0, u).astype(jnp.bfloat16)
        prb = gathered(sp, 0, u)
        rhs = jnp.concatenate([jnp.where(low, prb, 0.0), jnp.where(low, 0.0, prb)], axis=0)
        both = jnp.dot(lhs, rhs.astype(jnp.bfloat16), preferred_element_type=jnp.float32)
        both = both.astype(jnp.bfloat16)
        solved[r0 + u] = both
        solved[r0 + 16 + u] = jnp.concatenate([both[:, BLOCK:], both[:, :BLOCK]], axis=1)

    def couple_spread(g, sc, q):
        kp, p = q // 32, q % 32
        r0 = pl.multiple_of(g * 16, 16)
        spread(cpl_v, r0, 2 * ROW * kp, r0, 2 * ROW * kp + ROW, sc, 16 * BLOCK * kp, p)

    def couple(g, sc, up):
        parts = []
        for e in range(2):
            u = up // 4 * 8 + up % 4 + 4 * e
            lhs = [gathered(sc, 16 * BLOCK * kp, u).astype(jnp.bfloat16) for kp in range(kb // 2)]
            rhs = [solved[cols[k, g * 16 + u] ^ (16 * e)] for k in range(kb)]
            parts.append(jnp.dot(jnp.concatenate(lhs, axis=1), jnp.concatenate(rhs, axis=0), preferred_element_type=jnp.float32))
        both = jnp.where(low, parts[0], parts[1]).astype(jnp.bfloat16)
        out_v[2 * g + up // 4, up % 4 * BLOCK : up % 4 * BLOCK + BLOCK, :] = both

    def out_copy(g):
        return pltpu.make_async_copy(out_v.at[pl.ds(2 * g, 2)], out_ref.at[pl.ds(2 * g, 2)], out_sem.at[g])

    def wait(g):
        for copy in interior_copies(g):
            copy.wait()

    def solve_beside(g, sa, sp, na, np_):
        for u in range(16):
            solve(g, sa, sp, u)
            solve_spread(g + 1, na, np_, 2 * u)

    wait(0)
    for p in range(0, BLOCK // 2, 2):
        solve_spread(0, a0, p0, p)

    def two_groups(t, carry):
        wait(2 * t + 1)
        wait(2 * t + 2)
        solve_beside(2 * t, a0, p0, a1, p1)
        solve_beside(2 * t + 1, a1, p1, a0, p0)
        return carry

    lax.fori_loop(0, groups // 2 - 1, two_groups, 0)
    wait(groups - 1)
    for g in range(cgroups):
        coupling_copy(g).wait()
    cols_copy.wait()
    solve_beside(groups - 2, a0, p0, a1, p1)
    for u in range(16):
        solve(groups - 1, a1, p1, u)
        for q in range(8 * u, 8 * u + 8, 2):
            couple_spread(0, c0, q)
    for g in range(cgroups):
        here, there = (c0, c1) if g % 2 == 0 else (c1, c0)
        for up in range(8):
            couple(g, here, up)
            if g + 1 < cgroups:
                for q in range(16 * up, 16 * up + 16, 2):
                    couple_spread(g + 1, there, q)
        out_copy(g).start()
    for g in range(cgroups):
        out_copy(g).wait()


def paired_pieces(block_inverse, probes, coupling, columns, regions):
    nb, ni = block_inverse.shape[0], coupling.shape[0]
    any_place = pl.BlockSpec(memory_space=pl.ANY)
    stage = pltpu.VMEM((16 * BLOCK, 128), jnp.float32)
    big = pltpu.VMEM((64 * BLOCK, 128), jnp.float32)
    return pl.pallas_call(
        pieces_kernel,
        out_shape=jax.ShapeDtypeStruct((regions, ni * BLOCK // regions // 2, 2 * RANK), jnp.bfloat16),
        in_specs=[any_place] * 4,
        out_specs=any_place,
        scratch_shapes=[
            pltpu.SMEM(columns.shape[::-1], jnp.int32),
            pltpu.VMEM(block_inverse.shape, jnp.bfloat16),
            pltpu.VMEM(probes.shape, jnp.bfloat16),
            pltpu.VMEM(coupling.shape, jnp.bfloat16),
            stage, stage, stage, stage, big, big,
            pltpu.VMEM((nb, BLOCK, 128), jnp.bfloat16),
            pltpu.VMEM((regions, ni * BLOCK // regions // 2, 2 * RANK), jnp.bfloat16),
            pltpu.SemaphoreType.DMA((3, nb // 32)),
            pltpu.SemaphoreType.DMA(()),
            pltpu.SemaphoreType.DMA((ni // 16,)),
        ],
        compiler_params=pltpu.CompilerParams(vmem_limit_bytes=58 * MIB),
    )(columns.T, block_inverse, probes, coupling)


def three_parts(x):
    high = x.astype(jnp.bfloat16)
    rest = x - high.astype(jnp.float32)
    middle = rest.astype(jnp.bfloat16)
    low = (rest - middle.astype(jnp.float32)).astype(jnp.bfloat16)
    return jnp.concatenate([high, middle, low], axis=0)


def packed_sums(gram, moment):
    half = gram.shape[0] // 2
    row_at = lax.broadcasted_iota(jnp.int32, (half, half), 0)
    lane_at = lax.broadcasted_iota(jnp.int32, (half, half), 1)
    first, corner, second = gram[:half, :half], gram[:half, half:], gram[half:, half:]
    square = jnp.concatenate([jnp.where(lane_at >= row_at, first, second), corner], axis=1)
    diagonal = jnp.sum(jnp.where(lane_at == row_at, second, 0.0), axis=0, keepdims=True)
    last = jnp.concatenate([moment, diagonal, jnp.zeros_like(diagonal)], axis=1)
    square = jnp.concatenate([square[: half // 2], square[half // 2 :]], axis=1)
    return [square[i : i + 1] for i in range(half // 2)] + [last]


def unpacked_sums(packed):
    lanes = 2 * RANK
    packed = jnp.concatenate([packed[:, i : i + lanes] for i in range(0, packed.shape[1], lanes)], axis=0)
    half = lanes // 4
    rank = 2 * half
    row_at = lax.broadcasted_iota(jnp.int32, (half, half), 0)
    lane_at = lax.broadcasted_iota(jnp.int32, (half, half), 1)
    square = jnp.concatenate([packed[: half // 2, :rank], packed[: half // 2, rank:]], axis=0)
    turned = jnp.transpose(jnp.concatenate([square, square], axis=1), (1, 0))
    upper, lower = square[:, :half], turned[:half]
    moment, diagonal = packed[half // 2 : half // 2 + 1, :rank], packed[half // 2 : half // 2 + 1, rank : rank + half]
    first = jnp.where(lane_at >= row_at, upper, lower)
    second = jnp.where(lane_at >= row_at, lower, upper)
    second = jnp.where(lane_at == row_at, diagonal, second)
    top = jnp.concatenate([first, square[:, half:]], axis=1)
    return jnp.concatenate([top, jnp.concatenate([turned[half:rank], second], axis=1)], axis=0), moment


def gram_kernel(pairs_ref, res_ref, sums_ref, turned_ref):
    regions, half, lanes = pairs_ref.shape
    rank = lanes // 2
    gram = jnp.zeros((lanes, lanes), jnp.float32)
    moment = jnp.zeros((6, lanes), jnp.float32)
    for r in range(regions):
        pairs = pairs_ref[r]
        at = 2 * r * half
        turned = jnp.transpose(pairs, (1, 0))
        turned_ref[:, at : at + half] = turned[:rank]
        turned_ref[:, at + half : at + 2 * half] = turned[rank:]
        gram += jnp.dot(turned, pairs, preferred_element_type=jnp.float32)
        parts = [three_parts(res_ref[:, at + half * i : at + half * i + half]) for i in range(2)]
        moment += jnp.dot(jnp.concatenate(parts, axis=0), pairs, preferred_element_type=jnp.float32)
    gram = gram[:rank, :rank] + gram[rank:, rank:]
    moment = moment[:3, :rank] + moment[3:, rank:]
    packed = packed_sums(gram, moment[0:1] + moment[1:2] + moment[2:3])
    for i, row in enumerate(packed):
        sums_ref[0, :, lanes * i : lanes * i + lanes] = row


def two_parts(x):
    high = x.astype(jnp.bfloat16)
    return jnp.concatenate([high, (x - high.astype(jnp.float32)).astype(jnp.bfloat16)], axis=0)


def inverse_lower(gram):
    rank = gram.shape[0]
    row_at = lax.broadcasted_iota(jnp.int32, (rank, 2 * rank), 0)
    lane_at = lax.broadcasted_iota(jnp.int32, (rank, 2 * rank), 1)
    rest = jnp.concatenate([gram, jnp.zeros_like(gram)], axis=1) + (lane_at == row_at + rank).astype(jnp.float32)
    done = []
    for k in range(0, rank, STEP):
        at = row_at[: rank - k]
        cols = [jnp.broadcast_to(rest[:, k + j : k + j + 1], rest.shape) for j in range(STEP)]
        rows = [rest[j : j + 1, :] for j in range(STEP)]
        pivots = []
        for j in range(STEP):
            pivot = cols[j][j : j + 1, :]
            pivots.append(pivot)
            factor = jnp.where(at > j, cols[j] * (1.0 / pivot), 0.0)
            for l in range(j + 1, STEP):
                cols[l] = cols[l] - factor * cols[l][j : j + 1, :]
                rows[l] = rows[l] - factor[l : l + 1, :] * rows[j]
            rest = rest - factor * rows[j]
        done.append(rest[:STEP, rank:] * lax.rsqrt(jnp.concatenate(pivots, axis=0)[:, :rank]))
        rest = rest[STEP:]
    return jnp.concatenate(done, axis=0)


def finish_kernel(total_rows, sums_ref, rows_ref, basis_ref, corr_ref, basis_v, sem):
    rank, run = rows_ref.shape[0], rows_ref.shape[1] // sem.shape[0]
    regions = sem.shape[0]
    total = sums_ref[0]
    for n in range(1, sums_ref.shape[0]):
        total = total + sums_ref[n]
    gram, moment = unpacked_sums(total)
    lower_inverse = inverse_lower(gram)
    coefficients = jnp.sum(lower_inverse * moment, axis=1, keepdims=True)
    weights = two_parts(lower_inverse * math.sqrt(total_rows))
    shrink = 1.0 / math.sqrt(rank)

    def copy_out(r):
        cols = pl.ds(r * run, run)
        return pltpu.make_async_copy(basis_v.at[:, cols], basis_ref.at[:, cols], sem.at[r])

    for r in range(regions):
        q = jnp.dot(weights, rows_ref[:, r * run : (r + 1) * run], preferred_element_type=jnp.float32)
        q = q[:rank] + q[rank:]
        basis_v[:, r * run : (r + 1) * run] = q
        copy_out(r).start()
        corr_ref[:, r * run : (r + 1) * run] = jnp.sum(q * (coefficients * shrink), axis=0, keepdims=True)
    for r in range(regions):
        copy_out(r).wait()


def per_device(block_inverse, probes, coupling, columns, residual):
    regions, subs = lax.axis_size("region"), lax.axis_size("sub")
    rows_here = residual.shape[0]
    in_vmem = pl.BlockSpec(memory_space=pltpu.VMEM)
    pieces = paired_pieces(block_inverse, probes, coupling, columns, regions)
    owned = lax.all_to_all(pieces, "region", split_axis=0, concat_axis=0, tiled=True)
    sums, turned = pl.pallas_call(
        gram_kernel,
        out_shape=(
            jax.ShapeDtypeStruct((1, 1, (RANK // 4 + 1) * 2 * RANK), jnp.float32),
            jax.ShapeDtypeStruct((RANK, rows_here), jnp.bfloat16),
        ),
        in_specs=[in_vmem, in_vmem],
        out_specs=(in_vmem, in_vmem),
        compiler_params=pltpu.CompilerParams(vmem_limit_bytes=16 * MIB),
    )(owned, residual.reshape(1, rows_here))
    near = subs // SUB_Y
    for step in (near, 3 * near):
        sums = sums + lax.ppermute(sums, "sub", [(i, i ^ step) for i in range(subs)])
    columns_z = [[near * y + z for z in range(near)] for y in range(SUB_Y)]
    sums = jnp.broadcast_to(sums, (near,) + sums.shape[1:])
    sums = lax.all_to_all(sums, "sub", split_axis=0, concat_axis=0, tiled=True, axis_index_groups=columns_z)
    basis_t, correction = pl.pallas_call(
        functools.partial(finish_kernel, rows_here * subs),
        out_shape=(
            jax.ShapeDtypeStruct((RANK, rows_here), jnp.float32),
            jax.ShapeDtypeStruct((1, rows_here), jnp.float32),
        ),
        in_specs=[in_vmem, in_vmem],
        out_specs=(pl.BlockSpec(memory_space=pl.ANY), in_vmem),
        scratch_shapes=[pltpu.VMEM((RANK, rows_here), jnp.float32), pltpu.SemaphoreType.DMA((regions,))],
        compiler_params=pltpu.CompilerParams(vmem_limit_bytes=16 * MIB),
    )(sums, turned)
    return basis_t.T, correction.reshape(rows_here)


def solution(mesh):
    blocks = P(("region", "sub"), None)
    rows = P(("region", "sub"))
    return jax.shard_map(
        per_device,
        mesh=mesh,
        in_specs=(blocks, blocks, blocks, blocks, rows),
        out_specs=(blocks, rows),
        check_vma=False,
    )
```
